32 devices in a mesh: dp: 8 (over z, x), fsdp: 4 (over y, core).
Axes of the slice: x: 2, y: 2, z: 4, core: 2. Of those that a mesh axis runs over, the one named last changes fastest.
Arguments:
- token_ids: int32 [32, 1024], P(('dp', 'fsdp')), may hold values from 0 to 31998
- mask_flags: int32 [32, 1024], P(('dp', 'fsdp')), may hold values from 0 to 1, as said below
- time_bins: int32 [32], P(('dp', 'fsdp')), may hold values from 0 to 7
- doc_lengths: int32 [32, 4], P(('dp', 'fsdp')), may hold values from 1 to 512, 1024 in all within a row
- layer_mats: float32 [2, 768, 9216], P(None, None, ('fsdp', 'dp'))
- mats_first: float32 [2, 768, 9216], P(None, None, ('fsdp', 'dp')), may hold values from -3.8146973e-06 to 3.8146973e-06
- mats_second: float32 [2, 768, 9216], P(None, None, ('fsdp', 'dp')), may hold values from 2.0787337e-12 to 8.308616e-12
- soap_bases: float32 [2, 4, 768, 768], replicated, as said below
- soap_stats: float32 [2, 4, 768, 768], replicated, as said below
- vocab_tables: float32 [2, 32000, 768], P(None, ('fsdp', 'dp'))
- tables_first: float32 [2, 32000, 768], P(None, ('fsdp', 'dp')), may hold values from -3.8146973e-06 to 3.8146973e-06
- tables_second: float32 [2, 32000, 768], P(None, ('fsdp', 'dp')), may hold values from 2.0787337e-12 to 8.308616e-12
- norm_gains: float32 [5, 768], replicated, may hold values from 0.5 to 1.5
- gains_first: float32 [5, 768], replicated, may hold values from -1.5258789e-05 to 1.5258789e-05
- gains_second: float32 [5, 768], replicated, may hold values from 3.325026e-11 to 1.3300104e-10
Outputs:
- loss_sum: float32 [], replicated
- mask_count: float32 [], replicated
- clip_norm: float32 [], replicated
- new_mats: float32 [2, 768, 9216], P(None, None, ('fsdp', 'dp'))
- new_mats_first: float32 [2, 768, 9216], P(None, None, ('fsdp', 'dp'))
- new_mats_second: float32 [2, 768, 9216], P(None, None, ('fsdp', 'dp'))
- new_bases: float32 [2, 4, 768, 768], replicated
- new_stats: float32 [2, 4, 768, 768], replicated
- new_tables: float32 [2, 32000, 768], P(None, ('fsdp', 'dp'))
- new_tables_first: float32 [2, 32000, 768], P(None, ('fsdp', 'dp'))
- new_tables_second: float32 [2, 32000, 768], P(None, ('fsdp', 'dp'))
- new_gains: float32 [5, 768], replicated
- new_gains_first: float32 [5, 768], replicated
- new_gains_second: float32 [5, 768], replicated
The draws below stay inside these ranges and needn't reach their ends.
Inputs may be any that keep to these rules, and one draw needn't show every extreme that they name: `mask_flags`: each row has between 1 and 256 masked positions, and in every draw some row has exactly 256. `soap_stats`: every [768, 768] statistic is symmetric positive definite. `soap_bases`: every [768, 768] basis is orthogonal.
All inputs are finite; a program needn't handle non-finite values.
Results may differ from the reference program's by a relative error of at most 0.0018.
The reference program's roundings to bfloat16 on the way count: a program that leaves them out, or rounds other values in their place, can miss the bound.
Values may be sent and summed in bfloat16 or wider, within the bound.
No kernel may reach another device: no remote copies, remote signals or barrier semaphores. Data moves between devices by JAX's collectives and lax.ppermute only.
A program may use at most 640 MiB of HBM per device.

```python
import math
import jax
import jax.numpy as jnp
import numpy as np
from jax import lax

D = 768
HEADS = 12
HD = 64
FF = 2048
V = 32000
LAYERS = 2
ROW = 1024
SLOTS = 256
DOCS = 4
BINS = 8
STEP = 10
WIDE = 9216
ROWS = 32


def draw_mask_flags(key, part):
    key = jax.random.fold_in(key, 1)
    key_jitter, key_order = jax.random.split(key)
    row_rank = jnp.arange(ROWS, dtype=jnp.int32)
    jitter = jax.random.randint(key_jitter, (ROWS,), 0, max(SLOTS // 8, 1)) * (row_rank < ROWS - 1).astype(jnp.int32)
    counts = SLOTS - (ROWS - 1 - row_rank) * (2 * SLOTS // 3) // max(ROWS - 1, 1) - jitter
    counts = jnp.maximum(counts, 1)
    noise = jax.random.randint(key_order, (ROWS, ROW), 0, 1 << 20) * ROW + jnp.arange(ROW, dtype=jnp.int32)[None, :]
    ranking = jnp.argsort(jnp.argsort(noise, axis=1), axis=1)
    return (ranking < counts[:, None]).astype(jnp.int32)


def draw_layer_mats(key, part):
    key = jax.random.fold_in(key, 2)
    columns = jnp.arange(WIDE)
    scales = jnp.where(columns < 3 * D, D ** (-0.5), jnp.where(columns < 4 * D, (ROW / DOCS) ** 0.5 * D ** (-0.5), jnp.where(columns < 4 * D + 2 * FF, D ** (-0.5), 2.0 * FF ** (-0.5))))
    base = jax.random.normal(key, (LAYERS, D, WIDE), jnp.float32)
    return base * scales


def draw_vocab_tables(key, part):
    key = jax.random.fold_in(key, 3)
    key_embed, key_head = jax.random.split(key)
    spread = 2.0
    embed = jax.random.normal(key_embed, (V, D), jnp.float32)
    head = jax.random.normal(key_head, (V, D), jnp.float32)
    rising = 1.0 + spread * jnp.arange(V, dtype=jnp.float32)[:, None] / V
    return jnp.stack([embed, head * rising * D ** (-0.5)])


def one_basis(key):
    basis = jnp.eye(D, dtype=jnp.float32)
    for sweep_at in range(16):
        key_perm, key_angle = jax.random.split(jax.random.fold_in(key, sweep_at))
        shuffled = jax.random.permutation(key_perm, D)
        angles = jax.random.uniform(key_angle, (D // 2,), jnp.float32, -math.pi, math.pi)
        first_ids = shuffled[0::2]
        second_ids = shuffled[1::2]
        cosine = jnp.cos(angles)[:, None]
        sine_part = jnp.sin(angles)[:, None]
        upper_rows = basis[first_ids]
        lower_rows = basis[second_ids]
        basis = basis.at[first_ids].set(cosine * upper_rows - sine_part * lower_rows)
        basis = basis.at[second_ids].set(sine_part * upper_rows + cosine * lower_rows)
    return basis


def draw_soap_bases(key, part):
    key = jax.random.fold_in(key, 4)
    return jax.vmap(one_basis)(jax.random.split(key, LAYERS * 4)).reshape(LAYERS, 4, D, D)


def draw_soap_stats(key, part):
    key = jax.random.fold_in(key, 5)
    key_diag, key_off = jax.random.split(key)
    size_stat = 2.0 * FF * 0.0025 / (2 * V * D + LAYERS * D * WIDE)
    diagonal = jnp.exp(jax.random.uniform(key_diag, (LAYERS, 4, D), jnp.float32, 0.0, math.log(4.0)))
    noise = jax.random.normal(key_off, (LAYERS, 4, D, D), jnp.float32)
    symmetric = (noise + jnp.swapaxes(noise, -1, -2)) * 0.5 ** 0.5 * 0.25 * D ** (-0.5)
    return size_stat * (symmetric + diagonal[..., None] * jnp.eye(D, dtype=jnp.float32))


def place_ends(entries, key, low, top_value):
    longest = entries.shape.index(max(entries.shape))
    spots = []
    for shift in (0, 1):
        where = [jax.random.randint(jax.random.fold_in(key, axis), (), 0, length) for axis, length in enumerate(entries.shape)]
        where[longest] = (where[longest] + shift) % entries.shape[longest]
        spots.append(tuple(where))
    return entries.at[spots[0]].set(low).at[spots[1]].set(top_value)


def block_levels(own_key, extent, cuts, smallest, top_value):
    def one(dim, shards_of):
        heights = jax.random.uniform(jax.random.fold_in(jax.random.fold_in(own_key, 6), dim), (shards_of,), jnp.float32, smallest / len(cuts), top_value / len(cuts))
        return jnp.repeat(jnp.exp(heights), extent[dim] // shards_of).reshape((-1,) + (1,) * (len(extent) - dim - 1))

    loudness = one(*cuts[0])
    for cut in cuts[1:]:
        loudness = loudness * one(*cut)
    return loudness


def rank_bounds(amount, slope):
    portions = [(1 << 20) // math.isqrt(standing ** slope) + 1 for standing in range(1, amount + 1)]
    deviation = 1 + sum(portions) // (1 << 30)
    return np.cumsum(np.array([max(1, weight // deviation) for weight in portions]))


def ranked_ids(stream_key, extent, amount, lean):
    listing = rank_bounds(amount, lean)
    lot = jax.random.randint(jax.random.fold_in(stream_key, 1), extent, 0, int(listing[amount - 1]))
    standing = jnp.searchsorted(jnp.asarray(listing, jnp.int32), lot, side="right")
    return jax.random.permutation(jax.random.fold_in(stream_key, 2), amount)[standing].astype(jnp.int32)


def profile(amount, total, most, slope):
    portions = [(1 << 20) // math.isqrt(standing ** slope) + 1 for standing in range(2, amount + 1)]
    spare, given = total - most - (amount - 1), [1] * (amount - 1)
    while spare > 0:
        free = [i for i in range(amount - 1) if given[i] < most]
        pool, budget = sum([portions[i] for i in free]), spare
        for i in free:
            addition = min(most - given[i], max(1, budget * portions[i] // pool), spare)
            given[i] = given[i] + addition
            spare = spare - addition
    return np.array([most] + given)


def uneven(rng, amount, total, most, slope):
    if amount == 2:
        one = jax.random.randint(rng, (), max(1, total - most), min(most, total - 1) + 1)
        return jnp.stack([one, total - one])
    sizes = jnp.asarray(profile(amount, total, most, slope), jnp.int32)
    pairs = (amount - 1) // 2
    donor, sink = sizes[1:1 + 2 * pairs:2], sizes[2:2 + 2 * pairs:2]
    margin = jnp.minimum(donor - 1, most - sink)
    moved = jax.random.randint(jax.random.fold_in(rng, 1), (pairs,), 0, 1 << 20) % (margin + 1)
    sizes = sizes.at[1:1 + 2 * pairs:2].set(donor - moved).at[2:2 + 2 * pairs:2].set(sink + moved)
    return sizes[jax.random.permutation(jax.random.fold_in(rng, 2), amount)]


def centred(rng, shape, scale, bound, pieces=(), kind=jnp.bfloat16):
    level = block_levels(rng, shape, pieces, -0.22, 0.18) if pieces else 1.0
    result = jax.random.normal(rng, shape, jnp.float32) * scale * level
    return jnp.minimum(jnp.maximum(result, -bound), bound).astype(kind)


def setup_inputs(seed: int = 0) -> dict:
    splits = jax.random.split(jax.random.key(seed), 16)
    return {
        "token_ids": place_ends(ranked_ids(splits[0], (ROWS, ROW), V - 1, 2), jax.random.fold_in(splits[0], 3), 0, (V - 1) - 1).astype(jnp.int32),
        "mask_flags": draw_mask_flags(jax.random.fold_in(splits[15], 71), 0),
        "time_bins": place_ends(jax.random.randint(splits[2], (ROWS,), 0, BINS), jax.random.fold_in(splits[2], 1), 0, BINS - 1).astype(jnp.int32),
        "doc_lengths": jax.vmap(lambda own: uneven(own, DOCS, ROW, ROW // 2, 1))(jax.random.split(splits[3], ROWS)).reshape((ROWS, DOCS)).astype(jnp.int32),
        "layer_mats": draw_layer_mats(jax.random.fold_in(splits[15], 71), 0),
        "mats_first": centred(splits[5], (LAYERS, D, WIDE), (0.00556 * (2 * V * D + LAYERS * D * WIDE) ** -0.5), 3.814697265625e-06, ((2, 32),), jnp.float32),
        "mats_second": jnp.clip(jnp.exp(math.log(8.308615948027231e-12) - 1.38553415 * jax.random.uniform(splits[6], (LAYERS, D, WIDE), jnp.float32) ** block_levels(splits[6], (LAYERS, D, WIDE), ((2, 32),), -0.2, 0.2)), 2.0787336695721192e-12, 8.308615948027231e-12),
        "soap_bases": draw_soap_bases(jax.random.fold_in(splits[15], 71), 0),
        "soap_stats": draw_soap_stats(jax.random.fold_in(splits[15], 71), 0),
        "vocab_tables": draw_vocab_tables(jax.random.fold_in(splits[15], 71), 0),
        "tables_first": centred(splits[10], (2, V, D), (0.00556 * (2 * V * D + LAYERS * D * WIDE) ** -0.5), 3.814697265625e-06, ((1, 32),), jnp.float32),
        "tables_second": jnp.clip(jnp.exp(math.log(8.308615948027231e-12) - 1.38553415 * jax.random.uniform(splits[11], (2, V, D), jnp.float32) ** block_levels(splits[11], (2, V, D), ((1, 32),), -0.2, 0.2)), 2.0787336695721192e-12, 8.308615948027231e-12),
        "norm_gains": jnp.clip(1.0 + 0.1 * jax.random.normal(splits[12], (2 * LAYERS + 1, D), jnp.float32), 0.5, 1.5),
        "gains_first": centred(splits[13], (2 * LAYERS + 1, D), (0.0222 * (2 * V * D + LAYERS * D * WIDE) ** -0.5), 1.52587890625e-05, (), jnp.float32),
        "gains_second": jnp.clip(jnp.exp(jax.random.uniform(splits[14], (2 * LAYERS + 1, D), jnp.float32, math.log(3.325026018408117e-11), math.log(1.3300104073632468e-10))), 3.325026018408117e-11, 1.3300104073632468e-10),
    }


@jax.custom_vjp
def low(v):
    return lax.optimization_barrier(v.astype(jnp.bfloat16)).astype(jnp.float32)

@jax.custom_vjp
def low_back(v):
    return v

def low_keep(v):
    return (low(v), None)

def low_pass(kept, grad):
    return (grad,)

def back_keep(v):
    return (v, None)

def back_low(kept, grad):
    return (low(grad),)
low.defvjp(low_keep, low_pass)
low_back.defvjp(back_keep, back_low)
highest = lax.Precision.HIGHEST
learn_rate = 0.05
beta_one = 0.9
beta_two = 0.95
eps_adam = 1e-08
decay_weight = 0.1
stat_decay = 0.95
clip_limit = 0.05
norm_eps = 1e-05

def rms_scale(values, gain):
    return values * lax.rsqrt(lax.optimization_barrier(jnp.mean(values * values, axis=-1, keepdims=True)) + norm_eps) * gain

def rotary(values, position, orientation):
    half_dim = values.shape[-1] // 2
    frequency = 10000.0 ** (-jnp.arange(half_dim, dtype=jnp.float32) / half_dim)
    angles = position[..., None].astype(jnp.float32) * frequency
    cosine = jnp.cos(angles)
    sine_part = orientation * jnp.sin(angles)
    first_half = values[..., :half_dim]
    second_half = values[..., half_dim:]
    return jnp.concatenate([first_half * cosine - second_half * sine_part, second_half * cosine + first_half * sine_part], axis=-1)

def split_heads(matrix):
    return matrix.reshape(matrix.shape[0], HEADS, HD).transpose(1, 0, 2)

def doc_layout(lengths):
    spots_all = jnp.arange(ROW, dtype=jnp.int32)
    ends_at = jnp.cumsum(lengths).astype(jnp.int32)
    passed = spots_all[:, None] >= ends_at[None, :]
    doc_index = lax.optimization_barrier(jnp.sum(passed.astype(jnp.int32), axis=1)).astype(jnp.int32)
    position = (spots_all - lax.optimization_barrier(jnp.sum(jnp.where(passed, lengths[None, :], 0), axis=1))).astype(jnp.int32)
    return (doc_index, position)

def slot_layout(masked_flags):
    spots_all = jnp.arange(ROW, dtype=jnp.int32)
    slot_order = jnp.argsort((1 - masked_flags) * ROW + spots_all)[:SLOTS].astype(jnp.int32)
    valid_slot = jnp.arange(SLOTS) < jnp.sum(masked_flags)
    return (slot_order, valid_slot)

def layer_forward(residual, weights, gain_pair, same_doc, position):
    normed = low(rms_scale(residual, gain_pair[0]))
    projected = low_back(jnp.dot(normed, weights[:, :3 * D], precision=highest))
    queries = low(rotary(split_heads(projected[:, :D]), position, 1.0))
    keys_turned = low(rotary(split_heads(projected[:, D:2 * D]), position, 1.0))
    values = low(split_heads(projected[:, 2 * D:]))
    scores = low_back(jnp.einsum('hqd,hkd->hqk', queries, keys_turned, precision=highest) * HD ** (-0.5))
    scores = jnp.where(same_doc[None], scores, -1000000000.0)
    softened = low(jax.nn.softmax(scores, axis=-1))
    attended = jnp.einsum('hqk,hkd->hqd', softened, values, precision=highest)
    attended = low(low_back(attended.transpose(1, 0, 2).reshape(-1, D)))
    middle = residual + low_back(jnp.dot(attended, weights[:, 3 * D:4 * D], precision=highest))
    normed_ffn = low(rms_scale(middle, gain_pair[1]))
    gate_up = low_back(jnp.dot(normed_ffn, weights[:, 4 * D:4 * D + 2 * FF], precision=highest))
    activated = low(jax.nn.silu(gate_up[:, :FF]) * gate_up[:, FF:])
    return middle + low_back(jnp.dot(activated, weights[:, 4 * D + 2 * FF:].T, precision=highest))

def row_loss(params, row_data):
    work_mats, work_tables, gains_all = params
    tokens, masked_flags, time_bin, lengths = row_data
    doc_index, position = doc_layout(lengths)
    same_doc = doc_index[:, None] == doc_index[None, :]
    residual = work_tables[0][jnp.where(masked_flags == 1, V - 1, tokens)]
    for layer_at in range(LAYERS):
        residual = layer_forward(residual, work_mats[layer_at], gains_all[2 * layer_at:2 * layer_at + 2], same_doc, position)
    slot_order, valid_slot = slot_layout(masked_flags)
    chosen = low(rms_scale(residual, gains_all[2 * LAYERS])[slot_order])
    logits = low_back(jnp.dot(chosen, work_tables[1].T, precision=highest))
    totals = jax.nn.logsumexp(logits, axis=-1)
    picked = jnp.take_along_axis(logits, tokens[slot_order][:, None], axis=1)[:, 0]
    weight = jnp.where(valid_slot, BINS / (time_bin + 1.0), 0.0)
    return jnp.sum(weight * (totals - picked))

def total_loss(params, rows_all):
    work = (low(params[0]), low(params[1]), params[2])

    def one_row(carry, row_data):
        return (carry + jax.checkpoint(row_loss)(work, row_data), None)
    total, _ = lax.scan(one_row, jnp.zeros((), jnp.float32), rows_all)
    return total

def adam_update(weight, grad, first, second):
    first = beta_one * first + (1.0 - beta_one) * grad
    second = beta_two * second + (1.0 - beta_two) * grad * grad
    heading = first / (1.0 - beta_one ** STEP) / (jnp.sqrt(second / (1.0 - beta_two ** STEP)) + eps_adam)
    return (weight - learn_rate * (heading + decay_weight * weight), first, second)

def renew_basis(statistic, basis):
    product = jnp.dot(statistic, basis, precision=highest)
    gram = jnp.dot(product.T, product, precision=highest)
    lower_factor = jnp.linalg.cholesky(gram)
    return jax.scipy.linalg.solve_triangular(lower_factor, product.T, lower=True).T

def reference(token_ids, mask_flags, time_bins, doc_lengths, layer_mats, mats_first, mats_second, soap_bases, soap_stats, vocab_tables, tables_first, tables_second, norm_gains, gains_first, gains_second):
    rows_all = (token_ids, mask_flags, time_bins, doc_lengths)
    loss_sum, pull = jax.vjp(lambda params: total_loss(params, rows_all), (layer_mats, vocab_tables, norm_gains))
    grad_mats, grad_tables, grad_gains = pull(jnp.ones((), jnp.float32))[0]
    mask_count = jnp.sum(mask_flags).astype(jnp.float32)
    squares = jnp.sum(grad_mats * grad_mats) + jnp.sum(grad_tables * grad_tables) + jnp.sum(grad_gains * grad_gains)
    clip_norm = jnp.sqrt(squares) / mask_count
    factor = jnp.minimum(1.0, clip_limit / clip_norm) / mask_count
    bounds = (0, 3 * D, 4 * D, 4 * D + 2 * FF, WIDE)
    mats_out, first_out, second_out, bases_out, stats_out = ([], [], [], [], [])
    for layer_at in range(LAYERS):
        mats_row, first_row, second_row, bases_row, stats_row = ([], [], [], [], [])
        for kind_at in range(4):
            low_col, high_col = (bounds[kind_at], bounds[kind_at + 1])
            clipped = grad_mats[layer_at, :, low_col:high_col] * factor
            basis = soap_bases[layer_at, kind_at]
            turned = jnp.dot(basis.T, clipped, precision=highest)
            first = beta_one * mats_first[layer_at, :, low_col:high_col] + (1.0 - beta_one) * turned
            second = beta_two * mats_second[layer_at, :, low_col:high_col] + (1.0 - beta_two) * turned * turned
            heading = first / (1.0 - beta_one ** STEP) / (jnp.sqrt(second / (1.0 - beta_two ** STEP)) + eps_adam)
            weight = layer_mats[layer_at, :, low_col:high_col]
            mats_row.append(weight - learn_rate * (jnp.dot(basis, heading, precision=highest) + decay_weight * weight))
            first_row.append(first)
            second_row.append(second)
            statistic = stat_decay * soap_stats[layer_at, kind_at] + (1.0 - stat_decay) * jnp.dot(clipped, clipped.T, precision=highest)
            stats_row.append(statistic)
            bases_row.append(renew_basis(statistic, basis))
        mats_out.append(jnp.concatenate(mats_row, axis=1))
        first_out.append(jnp.concatenate(first_row, axis=1))
        second_out.append(jnp.concatenate(second_row, axis=1))
        bases_out.append(jnp.stack(bases_row))
        stats_out.append(jnp.stack(stats_row))
    new_tables, new_tables_first, new_tables_second = adam_update(vocab_tables, grad_tables * factor, tables_first, tables_second)
    new_gains, new_gains_first, new_gains_second = adam_update(norm_gains, grad_gains * factor, gains_first, gains_second)
    return (loss_sum, mask_count, clip_norm, jnp.stack(mats_out), jnp.stack(first_out), jnp.stack(second_out), jnp.stack(bases_out), jnp.stack(stats_out), new_tables, new_tables_first, new_tables_second, new_gains, new_gains_first, new_gains_second)
```

```python
import jax
import jax.numpy as jnp
import numpy as np
from jax import lax
from jax.experimental import pallas as pl
from jax.experimental.pallas import tpu as pltpu
from jax.sharding import Mesh
from jax.sharding import PartitionSpec as P

D = 768
HEADS = 12
HD = 64
FF = 2048
V = 32000
LAYERS = 2
ROW = 1024
SLOTS = 256
BINS = 8
STEP = 10
WIDE = 9216
KINDS = 4
BOUNDS = (0, 3 * D, 4 * D, 4 * D + 2 * FF, WIDE)
CAP = 40
PAIR = 2 * HD
PAIRS = D // PAIR
BLOCK = 256
VMEM_CAP = 56 * 2**20
STEPS = 128
LIGHT = pl.CostEstimate(flops=1000, bytes_accessed=1000, transcendentals=0)
TILE = 8

bf16 = jnp.bfloat16
f32 = jnp.float32
highest = lax.Precision.HIGHEST
high = lax.Precision.HIGH
learn_rate = 0.05
beta_one = 0.9
beta_two = 0.95
eps_adam = 1e-08
decay_weight = 0.1
stat_decay = 0.95
clip_limit = 0.05
norm_eps = 1e-05

OWNERS = ("y", "c", "z", "x")
DATA = ("z", "x", "y", "c")
DP = ("z", "x")
FS = ("y", "c")
HEAD_GROUP = ("x", "y", "c")


def dot(a, b, dims, precision=None):
    return lax.dot_general(a, b, (dims, ((), ())), precision=precision, preferred_element_type=f32)


def nn(a, b, precision=None):
    return dot(a, b, ((1,), (0,)), precision)


def nt(a, b, precision=None):
    return dot(a, b, ((1,), (1,)), precision)


def tn(a, b, precision=None):
    return dot(a, b, ((0,), (0,)), precision)


def rms_scale(values, gain):
    return values * lax.rsqrt(jnp.mean(values * values, axis=-1, keepdims=True) + norm_eps) * gain


def silu_up(gate, up):
    return jax.nn.silu(gate) * up


def mm(a, b, ca, cb):
    return lax.dot_general(a, b, (((ca,), (cb,)), ((), ())), preferred_element_type=f32)


def rotate(x, cosine, sine, low_half):
    other = jnp.where(low_half, pltpu.roll(x, PAIR - HD // 2, 1), pltpu.roll(x, HD // 2, 1))
    return x * cosine + other * sine


def lane_masks():
    lane = lax.broadcasted_iota(jnp.int32, (1, PAIR), 1)
    return lane % HD < HD // 2, (lane < HD, lane >= HD)


def attend_kernel(q_ref, k_ref, v_ref, cq_ref, sq_ref, ck_ref, sk_ref, docq_ref, dock_ref,
                  out_ref, qs_ref, kt_ref, vb_ref, lse_ref):
    low_half, own = lane_masks()
    queries = rotate(q_ref[...], cq_ref[...], sq_ref[...], low_half).astype(bf16)
    qs_ref[...] = queries * jnp.asarray(HD ** (-0.5), bf16)
    keys = rotate(k_ref[...], ck_ref[...], sk_ref[...], low_half).astype(bf16)
    kt_ref[...] = keys
    values = v_ref[...]
    vb_ref[...] = values.astype(bf16)
    values_t = values.T.astype(bf16)
    dock = jnp.concatenate([dock_ref[...]] * (BLOCK // 128), axis=1)
    for at in range(0, q_ref.shape[0], BLOCK):
        rows = slice(at, at + BLOCK)
        same = dock == docq_ref[:, rows]
        outs = []
        for h in range(2):
            scores = mm(jnp.where(own[h], keys, 0), qs_ref[rows, :], 1, 1)
            scores = jnp.where(same, scores, -1000000000.0)
            top = jnp.max(scores, axis=0, keepdims=True)
            soft = jnp.exp(scores - top)
            total = jnp.sum(soft, axis=0, keepdims=True)
            lse_ref[0, h : h + 1, rows] = top + jnp.log(total)
            soft = (soft * (1.0 / total)).astype(bf16)
            outs.append(mm(values_t[h * HD : (h + 1) * HD], soft, 1, 0))
        out_ref[rows, :] = jnp.concatenate(outs, axis=0).T.astype(bf16)


def attend_back_kernel(qs_ref, k_ref, v_ref, g_ref, lse_ref, cq_ref, sq_ref, ck_ref, sk_ref, docq_ref, dock_ref,
                       dq_ref, dk_ref, dv_ref, dk_sum, dv_sum):
    low_half, own = lane_masks()
    keys, values = k_ref[...], v_ref[...]
    keys_t = keys.astype(f32).T.astype(bf16)
    dock = jnp.concatenate([dock_ref[...]] * (BLOCK // 128), axis=1)
    for at in range(0, qs_ref.shape[0], BLOCK):
        rows = slice(at, at + BLOCK)
        same = dock == docq_ref[:, rows]
        queries, grad = qs_ref[rows, :], g_ref[rows, :]
        back = []
        for h in range(2):
            scores = mm(jnp.where(own[h], keys, 0), queries, 1, 1)
            soft = jnp.exp(jnp.where(same, scores, -1000000000.0) - lse_ref[0, h : h + 1, rows])
            grad_soft = mm(jnp.where(own[h], values, 0), grad, 1, 1)
            delta = jnp.sum(soft * grad_soft, axis=0, keepdims=True)
            grad_scores = (soft * (grad_soft - delta)).astype(bf16)
            dv = mm(soft.astype(bf16), jnp.where(own[h], grad, 0), 1, 0)
            dk = mm(grad_scores, jnp.where(own[h], queries, 0), 1, 0)
            if at == 0 and h == 0:
                dv_sum[...] = dv
                dk_sum[...] = dk
            else:
                dv_sum[...] += dv
                dk_sum[...] += dk
            back.append(mm(keys_t[h * HD : (h + 1) * HD], grad_scores, 1, 0))
        dq = jnp.concatenate(back, axis=0).T * HD ** (-0.5)
        dq_ref[rows, :] = rotate(dq, cq_ref[rows, :], -sq_ref[rows, :], low_half).astype(bf16)
    dk_ref[...] = rotate(dk_sum[...], ck_ref[...], -sk_ref[...], low_half).astype(bf16)
    dv_ref[...] = dv_sum[...].astype(bf16)


def column(rows, shift=0):
    return pl.BlockSpec((rows, PAIR), lambda h: (0, h + shift))


def whole(shape):
    return pl.BlockSpec(shape, lambda h: (0,) * len(shape))


def stat_spec(rows):
    return pl.BlockSpec((1, 2, rows), lambda h: (h, 0, 0))


def attend(q, kv, turn_q, turn_k, doc_q, doc_k):
    n_q, n_k = q.shape[0], kv.shape[0]
    low = jax.ShapeDtypeStruct((n_q, D), bf16)
    low_k = jax.ShapeDtypeStruct((n_k, D), bf16)
    return pl.pallas_call(
        attend_kernel,
        grid=(PAIRS,),
        in_specs=[column(n_q), column(n_k), column(n_k, PAIRS)]
        + [whole((n_q, PAIR))] * 2 + [whole((n_k, PAIR))] * 2 + [whole((1, n_q)), whole((n_k, 128))],
        out_specs=[column(n_q), column(n_q), column(n_k), column(n_k), stat_spec(n_q)],
        out_shape=[low, low, low_k, low_k, jax.ShapeDtypeStruct((PAIRS, 2, n_q), f32)],
        compiler_params=pltpu.CompilerParams(vmem_limit_bytes=VMEM_CAP),
        cost_estimate=LIGHT,
        name="attend",
    )(q, kv, kv, *turn_q, *turn_k, doc_q, doc_k)


def attend_back(qs, k, v, grad, lse, turn_q, turn_k, doc_q, doc_k):
    n_q, n_k = qs.shape[0], k.shape[0]
    low = jax.ShapeDtypeStruct((n_q, D), bf16)
    low_k = jax.ShapeDtypeStruct((n_k, D), bf16)
    return pl.pallas_call(
        attend_back_kernel,
        grid=(PAIRS,),
        in_specs=[column(n_q), column(n_k), column(n_k), column(n_q), stat_spec(n_q)]
        + [whole((n_q, PAIR))] * 2 + [whole((n_k, PAIR))] * 2 + [whole((1, n_q)), whole((n_k, 128))],
        out_specs=[column(n_q), column(n_k), column(n_k)],
        out_shape=[low, low_k, low_k],
        scratch_shapes=[pltpu.VMEM((n_k, PAIR), f32)] * 2,
        compiler_params=pltpu.CompilerParams(vmem_limit_bytes=VMEM_CAP),
        cost_estimate=LIGHT,
        name="attend_back",
    )(qs, k, v, grad, lse, *turn_q, *turn_k, doc_q, doc_k)


def pair_tables(position):
    half = HD // 2
    frequency = 10000.0 ** (-jnp.arange(half, dtype=f32) / half)
    angles = position[:, None].astype(f32) * frequency
    cosine, sine = jnp.cos(angles), jnp.sin(angles)
    return jnp.concatenate([cosine] * 4, axis=1), jnp.concatenate([-sine, sine] * 2, axis=1)


def fm(a, b, ca, cb):
    return lax.dot_general(a, b, (((ca,), (cb,)), ((), ())), precision=highest, preferred_element_type=f32)


def inverse_factor(block):
    row_at = lax.broadcasted_iota(jnp.int32, (STEPS, STEPS), 0)
    col_at = lax.broadcasted_iota(jnp.int32, (STEPS, STEPS), 1)
    eye = jnp.where(row_at == col_at, 1.0, 0.0).astype(f32)
    sub = lax.broadcasted_iota(jnp.int32, (TILE, 1), 0)
    n = STEPS // TILE
    left = [block[i * TILE : (i + 1) * TILE] for i in range(n)]
    right = [eye[i * TILE : (i + 1) * TILE] for i in range(n)]
    for j in range(STEPS):
        at, within = divmod(j, TILE)
        row = left[at][within : within + 1]
        scale = 1.0 / row[:, j : j + 1]
        row = row * scale
        mate = right[at][within : within + 1] * scale
        for i in range(at, n):
            column = left[i][:, j : j + 1]
            if i == at:
                column = jnp.where(sub > within, column, 0.0)
            left[i] = left[i] - column * row
            right[i] = right[i] - column * mate
    upper = jnp.concatenate(left, axis=0)
    pivots = jnp.sum(jnp.where(row_at == col_at, upper, 0.0), axis=1, keepdims=True)
    return jnp.concatenate(right, axis=0) * lax.rsqrt(pivots)


def orthogonal_kernel(gram_ref, rows_ref, out_ref, rest):
    rest[...] = gram_ref[...]
    out_ref[...] = rows_ref[...]
    lane = lax.broadcasted_iota(jnp.int32, (1, D), 1)

    def body(b, _):
        start = pl.multiple_of(b * STEPS, STEPS)
        here = pl.ds(start, STEPS)
        inverse = inverse_factor(rest[here, here])
        upper = jnp.where(lane >= start + STEPS, fm(inverse, rest[here, :], 1, 0), 0.0)
        done = fm(out_ref[:, here], inverse, 1, 1)
        out_ref[...] -= fm(done, upper, 1, 0)
        out_ref[:, here] = done
        rest[...] -= fm(upper, upper, 0, 0)
        return 0

    lax.fori_loop(0, D // STEPS, body, 0)


def orthogonal_rows(gram, rows):
    return pl.pallas_call(
        orthogonal_kernel,
        out_shape=jax.ShapeDtypeStruct(rows.shape, f32),
        in_specs=[pl.BlockSpec(memory_space=pltpu.VMEM)] * 2,
        out_specs=pl.BlockSpec(memory_space=pltpu.VMEM),
        scratch_shapes=[pltpu.VMEM((D, D), f32)],
        compiler_params=pltpu.CompilerParams(vmem_limit_bytes=40 * 2**20),
        cost_estimate=LIGHT,
        name="orthogonal_rows",
    )(gram, rows)


def adam_update(weight, grad, first, second):
    first = beta_one * first + (1.0 - beta_one) * grad
    second = beta_two * second + (1.0 - beta_two) * grad * grad
    heading = (
        first / (1.0 - beta_one**STEP) / (jnp.sqrt(second / (1.0 - beta_two**STEP)) + eps_adam)
    )
    return (weight - learn_rate * (heading + decay_weight * weight), first, second)


def parts_of(weights):
    return (
        weights[: 3 * D],
        weights[3 * D : 4 * D],
        weights[4 * D : 4 * D + 2 * FF],
        weights[4 * D + 2 * FF :],
    )


def layer_forward(residual, slots, weights, gains, doc, tables):
    w_qkv, w_out, w_gu, w_down = parts_of(weights)
    normed = rms_scale(residual, gains[0]).astype(bf16)
    if slots is None:
        rows_in, normed_q, doc_q, tables_q = residual, normed, doc[0], tables
    else:
        pick, doc_q, tables_q = slots
        rows_in = nn(pick.astype(f32), residual, highest)
        normed_q = nn(pick, normed).astype(bf16)
    attended, *kept = attend(
        nt(normed_q, w_qkv[:D]), nt(normed, w_qkv[D:]), tables_q, tables, doc_q, doc[1]
    )
    middle = rows_in + nt(attended, w_out)
    normed_ffn = rms_scale(middle, gains[1]).astype(bf16)
    gate_up = nt(normed_ffn, w_gu)
    activated = silu_up(gate_up[:, :FF], gate_up[:, FF:]).astype(bf16)
    result = middle + nn(activated, w_down)
    saved = (residual, normed, normed_q, kept, attended, middle, normed_ffn, gate_up, activated)
    return result, saved


def ffn_back(grad_out, saved, weights, gains, between):
    _, _, w_gu, w_down = parts_of(weights)
    _, _, _, _, attended, middle, normed_ffn, gate_up, activated = saved
    grad_low = grad_out.astype(bf16)
    grad_down = tn(activated, grad_low)
    grad_act = nt(grad_low, w_down)
    _, pull_act = jax.vjp(silu_up, gate_up[:, :FF], gate_up[:, FF:])
    grad_gate_up = jnp.concatenate(pull_act(grad_act), axis=1).astype(bf16)
    grad_gate_up, grad_down = between((grad_gate_up, grad_down))
    grad_gu = tn(grad_gate_up, normed_ffn)
    _, pull_ffn = jax.vjp(rms_scale, middle, gains[1])
    grad_middle, grad_gain = pull_ffn(nn(grad_gate_up, w_gu))
    grad_middle = grad_out + grad_middle
    branch = grad_middle.astype(bf16)
    return grad_middle, branch, tn(branch, attended), grad_gu, grad_down, grad_gain


def attention_back(grad_middle, branch, saved, slots, weights, gains, doc, tables, before, between):
    w_qkv, w_out, _, _ = parts_of(weights)
    residual, normed, normed_q, kept, _, _, _, _, _ = saved
    grad_att = before(nn(branch, w_out).astype(bf16))
    if slots is None:
        doc_q, tables_q = doc[0], tables
    else:
        pick, doc_q, tables_q = slots
    qs, k, v, lse = kept
    grads = attend_back(qs, k, v, grad_att, lse, tables_q, tables, doc_q, doc[1])
    grad_q, grad_k, grad_v = between(grads)
    grad_qkv = jnp.concatenate([tn(grad_q, normed_q), tn(grad_k, normed), tn(grad_v, normed)], 0)
    grad_in = nn(grad_k, w_qkv[D : 2 * D]) + nn(grad_v, w_qkv[2 * D :])
    grad_in_q = nn(grad_q, w_qkv[:D])
    if slots is not None:
        grad_in_q = tn(pick.astype(f32), grad_in_q, highest)
        grad_middle = tn(pick.astype(f32), grad_middle, highest)
    _, pull_att = jax.vjp(rms_scale, residual, gains[0])
    grad_residual, grad_gain = pull_att(grad_in + grad_in_q)
    return grad_middle + grad_residual, grad_qkv, grad_gain


def renew_rows(statistic, basis, start, rows):
    product = nn(statistic, basis, highest)
    gram = tn(product, product, highest)
    return orthogonal_rows(gram, lax.dynamic_slice_in_dim(product, start, rows))


def make_shards(sizes):
    n_z, n_x, n_y, n_c = (sizes[a] for a in ("z", "x", "y", "c"))
    n_dp, n_fs = n_z * n_x, n_y * n_c
    n_dev = n_dp * n_fs
    per = V // n_dev
    cols = WIDE // n_dev
    span = WIDE // n_fs
    n_mats = LAYERS * KINDS
    stat_rows = D // n_dp
    sharing = n_dev // n_mats
    basis_rows = D // sharing
    kind_of = np.searchsorted(np.array(BOUNDS[1:]), np.arange(WIDE), side="right")
    kind_lo = [int(kind_of[f * span]) for f in range(n_fs)]
    kind_hi = [int(kind_of[(f + 1) * span - 1]) for f in range(n_fs)]
    slots_all = n_dev * CAP
    shape = (n_z, n_x, n_y, n_c)
    paired = n_x == 2 and n_y == 2 and n_c == 2 and n_dp == n_mats

    def moved(value, target):
        pairs = []
        for source in np.ndindex(n_z, n_x, n_y, n_c):
            dest = target(*source)
            if dest is not None:
                pairs.append((np.ravel_multi_index(source, shape), np.ravel_multi_index(dest, shape)))
        return lax.ppermute(value, DATA, [(int(s), int(d)) for s, d in pairs])

    def line_gather(own):
        if not paired:
            return lax.all_gather(own, "z", axis=0, tiled=True)
        at = lax.axis_index("z")
        places = jnp.zeros((2 * n_z - 1,) + own.shape, own.dtype).at[n_z - 1].set(own)
        up, down = own, own
        for k in range(1, n_z):
            up = moved(up, lambda z, x, y, c: (z + 1, x, y, c) if z + 1 < n_z else None)
            down = moved(down, lambda z, x, y, c: (z - 1, x, y, c) if z > 0 else None)
            places = places.at[n_z - 1 - k].set(up).at[n_z - 1 + k].set(down)
        return lax.dynamic_slice_in_dim(places, n_z - 1 - at, n_z, axis=0).reshape(-1, D)

    def take(value, axis, at):
        return lax.dynamic_index_in_dim(value, at, axis, keepdims=False)

    def z_line(value, inside):
        at = lax.axis_index("z")
        up, down = 0.0, 0.0
        for k in range(n_z - 1, 0, -1):
            up = value[jnp.minimum(at + k, n_z - 1)] + up
            down = value[jnp.maximum(at - k, 0)] + down
            up, down = yield (
                (up, lambda z, x, y, c: (z + 1, x, y, c) if inside(y, c) and z + k < n_z else None),
                (down, lambda z, x, y, c: (z - 1, x, y, c) if inside(y, c) and z >= k else None),
            )
        return value[at] + up + down

    def two_ways(value, cross_y, inside):
        half = value.shape[-2] // 2
        first, second = value[..., :half, :], value[..., half:, :]
        x = lax.axis_index("x")
        x_at = -3
        sent_x, sent_y = yield (
            (take(first, x_at, 1 - x), lambda z, x, y, c: (z, 1 - x, y, c) if inside(None, c) else None),
            cross_y(second),
        )
        first = take(first, x_at, x) + sent_x
        second = cross_y(second, sent_y)
        sent_x, sent_y = yield (
            (take(second, x_at, 1 - x), lambda z, x, y, c: (z, 1 - x, y, c) if inside(y, c) else None),
            cross_y(first),
        )
        first = cross_y(first, sent_y)
        second = take(second, x_at, x) + sent_x
        return (yield from z_line(jnp.concatenate([first, second], axis=-2), inside))

    def sum_all(value):
        c, y = lax.axis_index("c"), lax.axis_index("y")
        (sent,) = yield ((take(value, 1, 1 - c), lambda z, x, y, c: (z, x, y, 1 - c)),)
        value = take(value, 1, c) + sent

        def cross_y(part, sent=None):
            if sent is None:
                return take(part, 0, 1 - y), lambda z, x, y, c: (z, x, 1 - y, c)
            return take(part, 0, y) + sent

        return (yield from two_ways(value, cross_y, lambda y, c: True))

    def sum_at(value, y_at, c_at=None):
        c = lax.axis_index("c")
        if c_at is None:
            request = value[1 - c], lambda z, x, y, c: (z, x, y, 1 - c)
        else:
            request = value, lambda z, x, y, c: (z, x, y, c_at) if c != c_at else None
        (sent,) = yield (request,)
        value = (value[c] if c_at is None else value) + sent

        def inside(y, c):
            return (y is None or y == y_at) and (c_at is None or c == c_at)

        def cross_y(part, sent=None):
            if sent is None:
                return part, lambda z, x, y, c: (z, x, y_at, c) if y != y_at and inside(None, c) else None
            return part + sent

        return (yield from two_ways(value, cross_y, inside))

    class Lane:
        def __init__(self, steps):
            self.steps, self.done, self.flying = steps, False, []
            self.asks = next(steps)

        def land(self, landed):
            try:
                self.asks = self.steps.send(landed)
            except StopIteration as end:
                self.done, self.result = True, end.value

    def start(value, *lanes):
        lanes = [lane for lane in lanes if not lane.done]
        operands = [[operand for operand, _ in lane.asks] for lane in lanes]
        value, operands = lax.optimization_barrier((value, operands))
        for lane, each in zip(lanes, operands):
            lane.flying = [moved(operand, target) for operand, (_, target) in zip(each, lane.asks)]
        return value

    def tick(value, *lanes):
        lanes = [lane for lane in lanes if not lane.done]
        value, landed = lax.optimization_barrier((value, [lane.flying for lane in lanes]))
        for lane, each in zip(lanes, landed):
            lane.land(each)
        return start(value, *lanes)

    def stat_routes():
        rounds, taken = [], []
        for kind in range(KINDS):
            blocks = range(BOUNDS[kind] // cols, -(-BOUNDS[kind + 1] // cols))
            for share, part in enumerate(np.array_split(np.array(blocks), sharing)):
                for block in part:
                    r = 0
                    while r < len(rounds) and (block in taken[r] or (kind, share) in rounds[r].values()):
                        r += 1
                    if r == len(rounds):
                        rounds.append({})
                        taken.append(set())
                    rounds[r][int(block)] = (kind, share)
                    taken[r].add(block)
        masks = np.zeros((KINDS, sharing, len(rounds), cols), np.float32)
        for r, each in enumerate(rounds):
            for block, (kind, share) in each.items():
                masks[kind, share, r] = kind_of[block * cols : (block + 1) * cols] == kind
        return rounds, masks

    def gather_stat(own, layer_at):
        rounds, _ = stat_routes()
        received = []
        for each in rounds:

            def target(z, x, y, c, each=each):
                found = each.get((y * n_c + c) * n_dp + z * n_x + x)
                if found is None:
                    return None
                kind, share = found
                dp = layer_at * KINDS + kind
                return dp // n_x, dp % n_x, share // n_c, share % n_c

            received.append(moved(own, target))
        return received

    def share_stat(pieces, mask):
        columns = jnp.concatenate([piece * mask[r][:, None] for r, piece in enumerate(pieces)], axis=0)
        part = tn(columns, columns, highest)
        c = lax.axis_index("c")
        halves = part.reshape(2, D // 2, D)
        mine = take(halves, 0, c) + moved(take(halves, 0, 1 - c), lambda z, x, y, c: (z, x, y, 1 - c))
        mine = mine + moved(mine, lambda z, x, y, c: (z, x, 1 - y, c))
        other = moved(mine, lambda z, x, y, c: (z, x, y, 1 - c))
        return jnp.where(c == 0, jnp.concatenate([mine, other], 0), jnp.concatenate([other, mine], 0))

    def shards(
        token_ids,
        mask_flags,
        time_bins,
        doc_lengths,
        layer_mats,
        mats_first,
        mats_second,
        soap_bases,
        soap_stats,
        vocab_tables,
        tables_first,
        tables_second,
        norm_gains,
        gains_first,
        gains_second,
    ):
        tokens, flags, lengths = token_ids[0], mask_flags[0], doc_lengths[0]
        work_mats = layer_mats.astype(bf16).transpose(0, 2, 1)
        work_tables = vocab_tables.astype(bf16)
        spots = jnp.arange(ROW, dtype=jnp.int32)

        ids = jnp.where(flags == 1, V - 1, tokens)
        owner = ids // per
        same_id = ids[:, None] == ids[None, :]
        before = spots[None, :] < spots[:, None]
        is_first = ~jnp.any(same_id & before, axis=1)
        place = jnp.sum(
            (before & is_first[None, :] & (owner[:, None] == owner[None, :])).astype(jnp.int32), axis=1
        )
        place = jnp.sum(jnp.where(same_id & is_first[None, :], place[None, :], 0), axis=1)
        mats_0 = lax.all_gather(work_mats[0], OWNERS, axis=0, tiled=True)
        slot_ids = jnp.arange(slots_all, dtype=jnp.int32)
        row_ids = jnp.arange(per, dtype=jnp.int32)

        def plan(turn_at):
            at = place - turn_at * CAP
            slot = jnp.where((at >= 0) & (at < CAP), owner * CAP + at, -1)
            hit = slot[:, None] == slot_ids[None, :]
            asked = jnp.max(jnp.where(hit, ids[:, None] % per, -1), axis=0).reshape(n_dev, CAP)
            most = jnp.broadcast_to(jnp.max(place), (n_dev, 128 - CAP))
            asked = jnp.concatenate([asked, most], axis=1)
            asked = lax.all_to_all(asked, OWNERS, 0, 0, tiled=True)
            rows = asked[:, :CAP].reshape(-1)[:, None] == row_ids[None, :]
            return hit, rows, jnp.max(asked[:, CAP]) // CAP + 1

        def fetch(hit, rows):
            sent = nn(rows.astype(bf16), work_tables[0]).astype(bf16)
            got = lax.all_to_all(sent, OWNERS, 0, 0, tiled=True)
            return nn(hit.astype(bf16), got)

        def embed_send(hit, grad):
            return tn(hit.astype(f32), grad, high)

        def exchange(sent):
            return lax.all_to_all(sent, OWNERS, 0, 0, tiled=True)

        def embed_sum(rows, got):
            return tn(rows.astype(f32), got, high)

        def fetch_more(turn_at, residual):
            hit, rows, _ = plan(turn_at)
            return residual + fetch(hit, rows)

        def give_more(turn_at, carry):
            total, grad = carry
            hit, rows, _ = plan(turn_at)
            return total + embed_sum(rows, exchange(embed_send(hit, grad))), grad

        hit_0, rows_0, rounds = plan(0)
        residual = fetch(hit_0, rows_0)
        residual = lax.fori_loop(1, rounds, fetch_more, residual)

        at_fs = lax.axis_index(FS)
        lo = jnp.asarray(kind_lo, jnp.int32)[at_fs]
        hi = jnp.asarray(kind_hi, jnp.int32)[at_fs]
        col_ids = (at_fs * n_dp + lax.axis_index(DP)) * cols + jnp.arange(cols, dtype=jnp.int32)
        kind_ids = sum((col_ids >= b).astype(jnp.int32) for b in BOUNDS[1:-1])
        in_lo = kind_ids == lo

        def stat_scatter(own):
            part = jnp.concatenate(
                [tn(jnp.where(in_lo[:, None], own, 0.0), own, highest), tn(jnp.where(in_lo[:, None], 0.0, own), own, highest)],
                axis=0,
            ).reshape(2, D, D)
            every = jnp.stack(
                [jnp.where(lo == kind, part[0], jnp.where(hi == kind, part[1], 0.0)) for kind in range(KINDS)]
            ).reshape(KINDS * D, D)
            return lax.psum_scatter(every, DATA, scatter_dimension=0, tiled=True)

        ends = jnp.cumsum(lengths)
        passed = spots[:, None] >= ends[None, :]
        doc = jnp.sum(passed.astype(jnp.int32), axis=1)
        position = spots - jnp.sum(jnp.where(passed, lengths[None, :], 0), axis=1)
        tables = pair_tables(position)
        docs = (doc[None, :], jnp.broadcast_to(doc[:, None], (ROW, 128)))

        count = jnp.sum(flags)
        order = jnp.where(flags == 1, jnp.cumsum(flags) - 1, count + jnp.cumsum(1 - flags) - 1)
        at_slot = order[None, :] == jnp.arange(SLOTS, dtype=jnp.int32)[:, None]
        pick = at_slot.astype(bf16)

        def picked(vector):
            return jnp.sum(jnp.where(at_slot, vector[None, :], jnp.zeros((), vector.dtype)), axis=1)

        targets = picked(tokens)
        valid = jnp.arange(SLOTS, dtype=jnp.int32) < count
        code = jnp.where(valid, time_bins[0] + 1, 0)
        slots = (pick, picked(doc)[None, :], pair_tables(picked(position)))

        group_codes = lax.all_gather(jnp.stack([targets, code]), HEAD_GROUP, axis=1, tiled=True)
        group_targets, group_codes = group_codes[0], group_codes[1]

        mats_1 = lax.all_gather(work_mats[1], OWNERS, axis=0, tiled=True)
        head = line_gather(work_tables[1])

        residual, saved_0 = layer_forward(residual, None, mats_0, norm_gains[0:2], docs, tables)
        final, saved_1 = layer_forward(residual, slots, mats_1, norm_gains[2:4], docs, tables)

        chosen_full, pull_final = jax.vjp(rms_scale, final, norm_gains[2 * LAYERS])
        states = lax.all_gather(chosen_full.astype(bf16), HEAD_GROUP, axis=0, tiled=True)
        logits = nt(states, head)
        base_shard = lax.axis_index(FS) * n_dp + lax.axis_index("x")
        vocab_ids = (
            (base_shard + jnp.arange(n_z, dtype=jnp.int32) * n_x)[:, None] * per + row_ids[None, :]
        ).reshape(-1)
        onehot = vocab_ids[None, :] == group_targets[:, None]
        top = jnp.max(logits, axis=1)
        total = jnp.sum(jnp.exp(logits - top[:, None]), axis=1)
        hit_logit = jnp.sum(jnp.where(onehot, logits, 0.0), axis=1)
        each = lax.all_gather(jnp.stack([top, total, hit_logit]), HEAD_GROUP, axis=0)
        top_all = jnp.max(each[:, 0], axis=0)
        log_total = top_all + jnp.log(jnp.sum(each[:, 1] * jnp.exp(each[:, 0] - top_all), axis=0))
        target_logit = jnp.sum(each[:, 2], axis=0)
        weight = jnp.where(group_codes > 0, BINS / jnp.maximum(group_codes, 1).astype(f32), 0.0)
        own_start = lax.axis_index(HEAD_GROUP) * SLOTS
        loss_part = jnp.sum(
            lax.dynamic_slice_in_dim(weight * (log_total - target_logit), own_start, SLOTS)
        )
        grad_logits = (
            weight[:, None] * (jnp.exp(logits - log_total[:, None]) - onehot.astype(f32))
        ).astype(bf16)
        grad_states = lax.psum_scatter(nn(grad_logits, head), HEAD_GROUP, scatter_dimension=0, tiled=True)
        head_part = tn(grad_logits, states)
        grad_states, head_part = lax.optimization_barrier((grad_states, head_part))
        grad_head = lax.psum_scatter(head_part, "z", scatter_dimension=0, tiled=True)
        grad_final, grad_final_gain = pull_final(grad_states)

        def same(value):
            return value

        middle_1, branch, out_1, gu_1, down_1, gain_f1 = ffn_back(
            grad_final, saved_1, mats_1, norm_gains[2:4], same
        )
        grad_1, qkv_1, gain_a1 = attention_back(
            middle_1, branch, saved_1, slots, mats_1, norm_gains[2:4], docs, tables, same, same
        )
        all_1 = jnp.concatenate([qkv_1, out_1, gu_1, down_1], axis=0)
        if paired:
            blocks = (n_z, n_x, cols, D)
            kept_head = [grad_head]

            def land_head(value):
                value, kept_head[0] = lax.optimization_barrier((value, kept_head[0]))
                return tick(value, lane_1)

            lane_1 = Lane(sum_all(all_1.reshape((n_y, n_c) + blocks)))
            grad_1 = start(grad_1, lane_1)
            middle_0, branch, out_0, gu_0, down_0, gain_f0 = ffn_back(
                grad_1, saved_0, mats_0, norm_gains[0:2], lambda v: tick(v, lane_1)
            )
            cut = span - D
            early_2 = Lane(sum_at(jnp.concatenate([out_0, gu_0[:cut]], axis=0).reshape(blocks), 0, 1))
            early_1 = Lane(sum_at(jnp.concatenate([gu_0[cut:], down_0], axis=0).reshape((n_c,) + blocks), 1))
            middle_0, branch = start((middle_0, branch), early_1, early_2)
            grad_0, qkv_0, gain_a0 = attention_back(
                middle_0, branch, saved_0, None, mats_0, norm_gains[0:2], docs, tables,
                lambda v: tick(v, early_1, early_2), land_head,
            )
            late = Lane(sum_at(qkv_0.reshape(blocks), 0, 0))
            sent = embed_send(hit_0, grad_0)
            grad_0, sent = start((grad_0, sent), late)
            embed_got = exchange(sent)
            lanes = (late, lane_1, early_1, early_2)
            tick(grad_0, *lanes)
            while not lane_1.done:
                tick(grad_0, *lanes)
            own_1 = lane_1.result
            pieces_1 = gather_stat(own_1, 1)
            tick(grad_0, *lanes)
            embed_got, pieces_1 = lax.optimization_barrier((embed_got, pieces_1))
            while not all(lane.done for lane in lanes):
                tick(grad_0, *lanes)
            y, c = lax.axis_index("y"), lax.axis_index("c")
            own_0 = jnp.where(y == 1, early_1.result, jnp.where(c == 1, early_2.result, late.result))
            grad_head = kept_head[0]
            pieces_0 = gather_stat(own_0, 0)
        else:
            own_1 = lax.psum_scatter(all_1, OWNERS, scatter_dimension=0, tiled=True)
            middle_0, branch, out_0, gu_0, down_0, gain_f0 = ffn_back(
                grad_1, saved_0, mats_0, norm_gains[0:2], same
            )
            grad_0, qkv_0, gain_a0 = attention_back(
                middle_0, branch, saved_0, None, mats_0, norm_gains[0:2], docs, tables, same, same
            )
            all_0 = jnp.concatenate([qkv_0, out_0, gu_0, down_0], axis=0)
            own_0 = lax.psum_scatter(all_0, OWNERS, scatter_dimension=0, tiled=True)
            embed_got, stat_1 = exchange(embed_send(hit_0, grad_0)), stat_scatter(own_1)
            stat_0 = stat_scatter(own_0)
        grad_embed = embed_sum(rows_0, embed_got)
        grad_embed, _ = lax.fori_loop(1, rounds, give_more, (grad_embed, grad_0))

        gain_part = jnp.stack([gain_a0, gain_f0, gain_a1, gain_f1, grad_final_gain])
        own_mats = jnp.stack([own_0, own_1])
        square = jnp.sum(own_mats * own_mats) + jnp.sum(grad_embed * grad_embed) + jnp.sum(grad_head * grad_head)
        scalars = jnp.stack([square, loss_part, count.astype(f32)])
        small = jnp.concatenate([gain_part, jnp.broadcast_to(scalars[:, None], (3, D))], axis=0)
        small = jnp.sum(lax.all_gather(small, DATA, axis=0), axis=0)
        gain_sum = small[: 2 * LAYERS + 1]
        square_sum, loss_sum, mask_count = (small[2 * LAYERS + 1 + i, 0] for i in range(3))
        clip_norm = jnp.sqrt(square_sum + jnp.sum(gain_sum * gain_sum)) / mask_count
        factor = jnp.minimum(1.0, clip_limit / clip_norm) / mask_count

        at_dp = lax.axis_index(DP)
        stat_scale = (1.0 - stat_decay) * (factor * factor)
        own_mat = at_dp * n_mats // n_dp
        linear = at_dp * n_fs + at_fs
        basis_start = (linear % sharing) * basis_rows
        flat_stats = soap_stats.reshape(n_mats, D, D)
        if paired:
            mask = jnp.asarray(stat_routes()[1])[own_mat % KINDS, at_fs]
            own_sum = share_stat([a + b for a, b in zip(pieces_0, pieces_1)], mask)
        else:
            own_sum = jnp.concatenate(
                [lax.all_gather(part, DATA, axis=0, tiled=True) for part in (stat_0, stat_1)], axis=0
            ).reshape(n_mats, D, D)[own_mat]
        own_stat = stat_decay * flat_stats[own_mat] + stat_scale * own_sum
        stats_part = lax.dynamic_slice_in_dim(own_stat, basis_start, basis_rows)
        new_stats = lax.all_gather(stats_part, DATA, axis=0, tiled=True).reshape(soap_stats.shape)
        own_basis = soap_bases.reshape(n_mats, D, D)[own_mat]
        new_rows = renew_rows(own_stat, own_basis, basis_start, basis_rows)
        new_bases = lax.all_gather(new_rows, DATA, axis=0, tiled=True).reshape(soap_bases.shape)

        clipped = own_mats * factor
        basis_lo = jnp.take(soap_bases, lo, axis=1)
        basis_hi = jnp.take(soap_bases, hi, axis=1)

        def by_kind(form, value):
            first = jnp.einsum(form, basis_lo, value, precision=highest)
            second = jnp.einsum(form, basis_hi, value, precision=highest)
            return jnp.where(in_lo[None, None, :], first, second)

        turned = by_kind("lij,lci->ljc", clipped)
        new_mats_first = beta_one * mats_first + (1.0 - beta_one) * turned
        new_mats_second = beta_two * mats_second + (1.0 - beta_two) * turned * turned
        heading = (
            new_mats_first
            / (1.0 - beta_one**STEP)
            / (jnp.sqrt(new_mats_second / (1.0 - beta_two**STEP)) + eps_adam)
        )
        direction = by_kind("lij,ljc->lic", heading)
        new_mats = layer_mats - learn_rate * (direction + decay_weight * layer_mats)
        new_tables, new_tables_first, new_tables_second = adam_update(
            vocab_tables, jnp.stack([grad_embed, grad_head]) * factor, tables_first, tables_second
        )
        new_gains, new_gains_first, new_gains_second = adam_update(
            norm_gains, gain_sum * factor, gains_first, gains_second
        )
        return (
            loss_sum,
            mask_count,
            clip_norm,
            new_mats,
            new_mats_first,
            new_mats_second,
            new_bases,
            new_stats,
            new_tables,
            new_tables_first,
            new_tables_second,
            new_gains,
            new_gains_first,
            new_gains_second,
        )

    return shards


def solution(mesh):
    n_dp, n_fs = mesh.shape["dp"], mesh.shape["fsdp"]
    n_x = 2 ** ((n_dp.bit_length() - 1) // 2)
    fine = Mesh(mesh.devices.reshape(n_dp // n_x, n_x, n_fs // 2, 2), ("z", "x", "y", "c"))
    rows, row = P(DATA, None), P(DATA)
    mats, tables = P(None, None, OWNERS), P(None, OWNERS, None)
    return jax.shard_map(
        make_shards(dict(fine.shape)),
        mesh=fine,
        in_specs=(rows, rows, row, rows, mats, mats, mats, P(), P(), tables, tables, tables, P(), P(), P()),
        out_specs=(P(), P(), P(), mats, mats, mats, P(), P(), tables, tables, tables, P(), P(), P()),
        check_vma=False,
    )
```

```python
import functools

import jax
import jax.numpy as jnp
import numpy as np
from jax import lax
from jax.experimental import pallas as pl
from jax.experimental.pallas import tpu as pltpu
from jax.sharding import Mesh
from jax.sharding import PartitionSpec as P

D = 768
HEADS = 12
HD = 64
FF = 2048
V = 32000
LAYERS = 2
ROW = 1024
SLOTS = 256
BINS = 8
STEP = 10
WIDE = 9216
KINDS = 4
BOUNDS = (0, 3 * D, 4 * D, 4 * D + 2 * FF, WIDE)
CAP = 40
PAIR = 2 * HD
PAIRS = D // PAIR
BLOCK = 256
VMEM_CAP = 56 * 2**20
STEPS = 128
LIGHT = pl.CostEstimate(flops=1000, bytes_accessed=1000, transcendentals=0)
TILE = 8

bf16 = jnp.bfloat16
f32 = jnp.float32
highest = lax.Precision.HIGHEST
high = lax.Precision.HIGH
learn_rate = 0.05
beta_one = 0.9
beta_two = 0.95
eps_adam = 1e-08
decay_weight = 0.1
stat_decay = 0.95
clip_limit = 0.05
norm_eps = 1e-05

OWNERS = ("y", "c", "z", "x")
DATA = ("z", "x", "y", "c")
DP = ("z", "x")
FS = ("y", "c")
HEAD_GROUP = ("z", "y", "c")


def dot(a, b, dims, precision=None):
    return lax.dot_general(a, b, (dims, ((), ())), precision=precision, preferred_element_type=f32)


def nn(a, b, precision=None):
    return dot(a, b, ((1,), (0,)), precision)


def nt(a, b, precision=None):
    return dot(a, b, ((1,), (1,)), precision)


def tn(a, b, precision=None):
    return dot(a, b, ((0,), (0,)), precision)


def rms_scale(values, gain):
    return values * lax.rsqrt(jnp.mean(values * values, axis=-1, keepdims=True) + norm_eps) * gain


def silu_up(gate, up):
    return jax.nn.silu(gate) * up


def mm(a, b, ca, cb):
    return lax.dot_general(a, b, (((ca,), (cb,)), ((), ())), preferred_element_type=f32)


def rotate(x, cosine, sine, low_half):
    other = jnp.where(low_half, pltpu.roll(x, PAIR - HD // 2, 1), pltpu.roll(x, HD // 2, 1))
    return x * cosine + other * sine


def lane_masks():
    lane = lax.broadcasted_iota(jnp.int32, (1, PAIR), 1)
    return lane % HD < HD // 2, (lane < HD, lane >= HD)


def attend_kernel(q_ref, k_ref, v_ref, cq_ref, sq_ref, ck_ref, sk_ref, docq_ref, dock_ref,
                  out_ref, qs_ref, kt_ref, vb_ref, lse_ref):
    low_half, own = lane_masks()
    queries = rotate(q_ref[...], cq_ref[...], sq_ref[...], low_half).astype(bf16)
    qs_ref[...] = queries * jnp.asarray(HD ** (-0.5), bf16)
    keys = rotate(k_ref[...], ck_ref[...], sk_ref[...], low_half).astype(bf16)
    kt_ref[...] = keys
    values = v_ref[...]
    vb_ref[...] = values.astype(bf16)
    values_t = values.T.astype(bf16)
    dock = jnp.concatenate([dock_ref[...]] * (BLOCK // 128), axis=1)
    for at in range(0, q_ref.shape[0], BLOCK):
        rows = slice(at, at + BLOCK)
        same = dock == docq_ref[:, rows]
        outs = []
        for h in range(2):
            scores = mm(jnp.where(own[h], keys, 0), qs_ref[rows, :], 1, 1)
            scores = jnp.where(same, scores, -1000000000.0)
            top = jnp.max(scores, axis=0, keepdims=True)
            soft = jnp.exp(scores - top)
            total = jnp.sum(soft, axis=0, keepdims=True)
            lse_ref[0, h : h + 1, rows] = top + jnp.log(total)
            soft = (soft * (1.0 / total)).astype(bf16)
            outs.append(mm(values_t[h * HD : (h + 1) * HD], soft, 1, 0))
        out_ref[rows, :] = jnp.concatenate(outs, axis=0).T.astype(bf16)


def attend_back_kernel(qs_ref, k_ref, v_ref, g_ref, lse_ref, cq_ref, sq_ref, ck_ref, sk_ref, docq_ref, dock_ref,
                       dq_ref, dk_ref, dv_ref, dk_sum, dv_sum):
    low_half, own = lane_masks()
    keys, values = k_ref[...], v_ref[...]
    keys_t = keys.astype(f32).T.astype(bf16)
    dock = jnp.concatenate([dock_ref[...]] * (BLOCK // 128), axis=1)
    for at in range(0, qs_ref.shape[0], BLOCK):
        rows = slice(at, at + BLOCK)
        same = dock == docq_ref[:, rows]
        queries, grad = qs_ref[rows, :], g_ref[rows, :]
        back = []
        for h in range(2):
            scores = mm(jnp.where(own[h], keys, 0), queries, 1, 1)
            soft = jnp.exp(jnp.where(same, scores, -1000000000.0) - lse_ref[0, h : h + 1, rows])
            grad_soft = mm(jnp.where(own[h], values, 0), grad, 1, 1)
            delta = jnp.sum(soft * grad_soft, axis=0, keepdims=True)
            grad_scores = (soft * (grad_soft - delta)).astype(bf16)
            dv = mm(soft.astype(bf16), jnp.where(own[h], grad, 0), 1, 0)
            dk = mm(grad_scores, jnp.where(own[h], queries, 0), 1, 0)
            if at == 0 and h == 0:
                dv_sum[...] = dv
                dk_sum[...] = dk
            else:
                dv_sum[...] += dv
                dk_sum[...] += dk
            back.append(mm(keys_t[h * HD : (h + 1) * HD], grad_scores, 1, 0))
        dq = jnp.concatenate(back, axis=0).T * HD ** (-0.5)
        dq_ref[rows, :] = rotate(dq, cq_ref[rows, :], -sq_ref[rows, :], low_half).astype(bf16)
    dk_ref[...] = rotate(dk_sum[...], ck_ref[...], -sk_ref[...], low_half).astype(bf16)
    dv_ref[...] = dv_sum[...].astype(bf16)


def column(rows, shift=0):
    return pl.BlockSpec((rows, PAIR), lambda h: (0, h + shift))


def whole(shape):
    return pl.BlockSpec(shape, lambda h: (0,) * len(shape))


def stat_spec(rows):
    return pl.BlockSpec((1, 2, rows), lambda h: (h, 0, 0))


def attend(q, kv, turn_q, turn_k, doc_q, doc_k):
    n_q, n_k = q.shape[0], kv.shape[0]
    low = jax.ShapeDtypeStruct((n_q, D), bf16)
    low_k = jax.ShapeDtypeStruct((n_k, D), bf16)
    return pl.pallas_call(
        attend_kernel,
        grid=(PAIRS,),
        in_specs=[column(n_q), column(n_k), column(n_k, PAIRS)]
        + [whole((n_q, PAIR))] * 2 + [whole((n_k, PAIR))] * 2 + [whole((1, n_q)), whole((n_k, 128))],
        out_specs=[column(n_q), column(n_q), column(n_k), column(n_k), stat_spec(n_q)],
        out_shape=[low, low, low_k, low_k, jax.ShapeDtypeStruct((PAIRS, 2, n_q), f32)],
        compiler_params=pltpu.CompilerParams(vmem_limit_bytes=VMEM_CAP),
        cost_estimate=LIGHT,
        name="attend",
    )(q, kv, kv, *turn_q, *turn_k, doc_q, doc_k)


def attend_back(qs, k, v, grad, lse, turn_q, turn_k, doc_q, doc_k):
    n_q, n_k = qs.shape[0], k.shape[0]
    low = jax.ShapeDtypeStruct((n_q, D), bf16)
    low_k = jax.ShapeDtypeStruct((n_k, D), bf16)
    return pl.pallas_call(
        attend_back_kernel,
        grid=(PAIRS,),
        in_specs=[column(n_q), column(n_k), column(n_k), column(n_q), stat_spec(n_q)]
        + [whole((n_q, PAIR))] * 2 + [whole((n_k, PAIR))] * 2 + [whole((1, n_q)), whole((n_k, 128))],
        out_specs=[column(n_q), column(n_k), column(n_k)],
        out_shape=[low, low_k, low_k],
        scratch_shapes=[pltpu.VMEM((n_k, PAIR), f32)] * 2,
        compiler_params=pltpu.CompilerParams(vmem_limit_bytes=VMEM_CAP),
        cost_estimate=LIGHT,
        name="attend_back",
    )(qs, k, v, grad, lse, *turn_q, *turn_k, doc_q, doc_k)


def pair_tables(position):
    half = HD // 2
    frequency = 10000.0 ** (-jnp.arange(half, dtype=f32) / half)
    angles = position[:, None].astype(f32) * frequency
    cosine, sine = jnp.cos(angles), jnp.sin(angles)
    return jnp.concatenate([cosine] * 4, axis=1), jnp.concatenate([-sine, sine] * 2, axis=1)


def fm(a, b, ca, cb):
    return lax.dot_general(a, b, (((ca,), (cb,)), ((), ())), precision=highest, preferred_element_type=f32)


def inverse_factor(block):
    row_at = lax.broadcasted_iota(jnp.int32, (STEPS, STEPS), 0)
    col_at = lax.broadcasted_iota(jnp.int32, (STEPS, STEPS), 1)
    eye = jnp.where(row_at == col_at, 1.0, 0.0).astype(f32)
    sub = lax.broadcasted_iota(jnp.int32, (TILE, 1), 0)
    n = STEPS // TILE
    left = [block[i * TILE : (i + 1) * TILE] for i in range(n)]
    right = [eye[i * TILE : (i + 1) * TILE] for i in range(n)]
    for j in range(STEPS):
        at, within = divmod(j, TILE)
        row = left[at][within : within + 1]
        scale = 1.0 / row[:, j : j + 1]
        row = row * scale
        mate = right[at][within : within + 1] * scale
        for i in range(at, n):
            column = left[i][:, j : j + 1]
            if i == at:
                column = jnp.where(sub > within, column, 0.0)
            left[i] = left[i] - column * row
            right[i] = right[i] - column * mate
    upper = jnp.concatenate(left, axis=0)
    pivots = jnp.sum(jnp.where(row_at == col_at, upper, 0.0), axis=1, keepdims=True)
    return jnp.concatenate(right, axis=0) * lax.rsqrt(pivots)


def orthogonal_kernel(steps, gram_ref, rows_ref, out_ref, rest_ref):
    rest_ref[...] = gram_ref[...]
    out_ref[...] = rows_ref[...]
    lane = lax.broadcasted_iota(jnp.int32, (1, gram_ref.shape[0]), 1)

    def body(b, _):
        start = pl.multiple_of(b * STEPS, STEPS)
        here = pl.ds(start, STEPS)
        inverse = inverse_factor(rest_ref[here, here])
        upper = jnp.where(lane >= start + STEPS, fm(inverse, rest_ref[here, :], 1, 0), 0.0)
        done = fm(out_ref[:, here], inverse, 1, 1)
        out_ref[...] -= fm(done, upper, 1, 0)
        out_ref[:, here] = done
        rest_ref[...] -= fm(upper, upper, 0, 0)
        return 0

    lax.fori_loop(0, steps, body, 0)


def orthogonal_rows(gram, rows, steps):
    return pl.pallas_call(
        functools.partial(orthogonal_kernel, steps),
        out_shape=[jax.ShapeDtypeStruct(rows.shape, f32), jax.ShapeDtypeStruct(gram.shape, f32)],
        in_specs=[pl.BlockSpec(memory_space=pltpu.VMEM)] * 2,
        out_specs=[pl.BlockSpec(memory_space=pltpu.VMEM)] * 2,
        compiler_params=pltpu.CompilerParams(vmem_limit_bytes=40 * 2**20),
        cost_estimate=pl.CostEstimate(flops=10**11, bytes_accessed=8 * D * D, transcendentals=0),
        name="orthogonal_rows",
    )(gram, rows)


def adam_update(weight, grad, first, second):
    first = beta_one * first + (1.0 - beta_one) * grad
    second = beta_two * second + (1.0 - beta_two) * grad * grad
    heading = (
        first / (1.0 - beta_one**STEP) / (jnp.sqrt(second / (1.0 - beta_two**STEP)) + eps_adam)
    )
    return (weight - learn_rate * (heading + decay_weight * weight), first, second)


def parts_of(weights):
    return (
        weights[: 3 * D],
        weights[3 * D : 4 * D],
        weights[4 * D : 4 * D + 2 * FF],
        weights[4 * D + 2 * FF :],
    )


def layer_forward(residual, slots, weights, gains, doc, tables):
    w_qkv, w_out, w_gu, w_down = parts_of(weights)
    normed = rms_scale(residual, gains[0]).astype(bf16)
    if slots is None:
        rows_in, normed_q, doc_q, tables_q = residual, normed, doc[0], tables
    else:
        pick, doc_q, tables_q = slots
        rows_in = nn(pick.astype(f32), residual, highest)
        normed_q = nn(pick, normed).astype(bf16)
    attended, *kept = attend(
        nt(normed_q, w_qkv[:D]), nt(normed, w_qkv[D:]), tables_q, tables, doc_q, doc[1]
    )
    middle = rows_in + nt(attended, w_out)
    normed_ffn = rms_scale(middle, gains[1]).astype(bf16)
    gate_up = nt(normed_ffn, w_gu)
    activated = silu_up(gate_up[:, :FF], gate_up[:, FF:]).astype(bf16)
    result = middle + nn(activated, w_down)
    saved = (residual, normed, normed_q, kept, attended, middle, normed_ffn, gate_up, activated)
    return result, saved


def ffn_back(grad_out, saved, weights, gains, cut, between):
    _, _, w_gu, w_down = parts_of(weights)
    _, _, _, _, attended, middle, normed_ffn, gate_up, activated = saved
    grad_low = grad_out.astype(bf16)
    grad_down = tn(activated, grad_low)
    grad_act = nt(grad_low, w_down)
    _, pull_act = jax.vjp(silu_up, gate_up[:, :FF], gate_up[:, FF:])
    grad_gate_up = jnp.concatenate(pull_act(grad_act), axis=1).astype(bf16)
    grad_gate_up, grad_down = between((grad_gate_up, grad_down))
    grad_gu = [tn(grad_gate_up[:, :cut], normed_ffn), tn(grad_gate_up[:, cut:], normed_ffn)]
    _, pull_ffn = jax.vjp(rms_scale, middle, gains[1])
    grad_middle, grad_gain = pull_ffn(nn(grad_gate_up, w_gu))
    grad_middle = grad_out + grad_middle
    branch = grad_middle.astype(bf16)
    return grad_middle, branch, tn(branch, attended), grad_gu, grad_down, grad_gain


def attention_back(grad_middle, branch, saved, slots, weights, gains, doc, tables, before, between):
    w_qkv, w_out, _, _ = parts_of(weights)
    residual, normed, normed_q, kept, _, _, _, _, _ = saved
    grad_att = before(nn(branch, w_out).astype(bf16))
    if slots is None:
        doc_q, tables_q = doc[0], tables
    else:
        pick, doc_q, tables_q = slots
    qs, k, v, lse = kept
    grads = attend_back(qs, k, v, grad_att, lse, tables_q, tables, doc_q, doc[1])
    grad_q, grad_k, grad_v = between(grads)
    grad_qkv = jnp.concatenate([tn(grad_q, normed_q), tn(grad_k, normed), tn(grad_v, normed)], 0)
    grad_in = nn(grad_k, w_qkv[D : 2 * D]) + nn(grad_v, w_qkv[2 * D :])
    grad_in_q = nn(grad_q, w_qkv[:D])
    if slots is not None:
        grad_in_q = tn(pick.astype(f32), grad_in_q, highest)
        grad_middle = tn(pick.astype(f32), grad_middle, highest)
    _, pull_att = jax.vjp(rms_scale, residual, gains[0])
    grad_residual, grad_gain = pull_att(grad_in + grad_in_q)
    return grad_middle + grad_residual, grad_qkv, grad_gain


def make_shards(sizes):
    n_z, n_x, n_y, n_c = (sizes[a] for a in ("z", "x", "y", "c"))
    n_dp, n_fs = n_z * n_x, n_y * n_c
    n_dev = n_dp * n_fs
    per = V // n_dev
    cols = WIDE // n_dev
    span = WIDE // n_fs
    n_mats = LAYERS * KINDS
    stat_rows = D // n_dp
    sharing = n_dev // n_mats
    basis_rows = D // sharing
    kind_of = np.searchsorted(np.array(BOUNDS[1:]), np.arange(WIDE), side="right")
    kind_lo = [int(kind_of[f * span]) for f in range(n_fs)]
    kind_hi = [int(kind_of[(f + 1) * span - 1]) for f in range(n_fs)]
    slots_all = n_dev * CAP
    shape = (n_z, n_x, n_y, n_c)
    paired = n_x == 2 and n_y == 2 and n_c == 2 and n_dp == n_mats

    def moved(value, target):
        pairs = []
        for source in np.ndindex(n_z, n_x, n_y, n_c):
            dest = target(*source)
            if dest is not None:
                pairs.append((np.ravel_multi_index(source, shape), np.ravel_multi_index(dest, shape)))
        return lax.ppermute(value, DATA, [(int(s), int(d)) for s, d in pairs])

    def take(value, axis, at):
        return lax.dynamic_index_in_dim(value, at, axis, keepdims=False)

    def z_line(value, inside):
        at = lax.axis_index("z")
        up, down = 0.0, 0.0
        for k in range(n_z - 1, 0, -1):
            up = value[jnp.minimum(at + k, n_z - 1)] + up
            down = value[jnp.maximum(at - k, 0)] + down
            up, down = yield (
                (up, lambda z, x, y, c: (z + 1, x, y, c) if inside(y, c) and z + k < n_z else None),
                (down, lambda z, x, y, c: (z - 1, x, y, c) if inside(y, c) and z >= k else None),
            )
        return value[at] + up + down

    def sum_all(value):
        c, y, x = lax.axis_index("c"), lax.axis_index("y"), lax.axis_index("x")
        rows = value.shape[-2] // 2

        def by_x(z, x, y, c):
            return z, 1 - x, y, c

        def by_y(z, x, y, c):
            return z, x, 1 - y, c

        kept = take(value, 1, c)
        (sent,) = yield ((take(value, 1, 1 - c), lambda z, x, y, c: (z, x, y, 1 - c)),)
        first = kept[..., :rows, :] + sent[..., :rows, :]
        second = kept[..., rows:, :] + sent[..., rows:, :]
        sent_x, sent_y = yield ((take(first, 2, 1 - x), by_x), (take(second, 0, 1 - y), by_y))
        first, second = take(first, 2, x) + sent_x, take(second, 0, y) + sent_y
        sent_y, sent_x = yield ((take(first, 0, 1 - y), by_y), (take(second, 1, 1 - x), by_x))
        first, second = take(first, 0, y) + sent_y, take(second, 1, x) + sent_x
        return (yield from z_line(jnp.concatenate([first, second], axis=-2), lambda y, c: True))

    class Lane:
        def __init__(self, steps):
            self.steps, self.done, self.flying = steps, False, []
            self.asks = next(steps)

        def land(self, landed):
            try:
                self.asks = self.steps.send(landed)
            except StopIteration as end:
                self.done, self.result = True, end.value

    def start(value, *lanes):
        lanes = [lane for lane in lanes if not lane.done]
        operands = [[operand for operand, _ in lane.asks] for lane in lanes]
        value, operands = lax.optimization_barrier((value, operands))
        for lane, each in zip(lanes, operands):
            lane.flying = [moved(operand, target) for operand, (_, target) in zip(each, lane.asks)]
        return value

    def tick(value, *lanes):
        lanes = [lane for lane in lanes if not lane.done]
        value, landed = lax.optimization_barrier((value, [lane.flying for lane in lanes]))
        for lane, each in zip(lanes, landed):
            lane.land(each)
        return start(value, *lanes)

    half = cols // 2
    has = [[(kind_of.reshape(n_fs, n_dp, cols) == kind)[f].any(axis=1) for f in range(n_fs)] for kind in range(KINDS)]
    merges = [n_fs == 4 and not any((has[k][y] & has[k][2 + y]).any() for y in range(2)) for k in range(KINDS)]
    work_axes = ("y", "z", "x", "c")

    def to_work(own):
        y, c = lax.axis_index("y"), lax.axis_index("c")
        pieces = own.reshape(1, 2, half, D) * (jnp.arange(2)[:, None, None, None] == c)
        got = lax.all_to_all(pieces.reshape(-1, D), FS, 0, 0, tiled=True).reshape(2, 2, half, D)
        return take(got, 1, y).reshape(-1, D)

    def from_work(work):
        y, c = lax.axis_index("y"), lax.axis_index("c")
        pieces = work.reshape(2, 1, half, D) * (jnp.arange(2)[None, :, None, None] == y)
        got = lax.all_to_all(pieces.reshape(-1, D), FS, 0, 0, tiled=True).reshape(2, 2, half, D)
        return take(got, 0, c).reshape(-1, D)

    def share_stat(columns):
        part = tn(columns, columns, highest)
        c = lax.axis_index("c")
        halves = part.reshape(2, D // 2, D)
        mine = take(halves, 0, c) + moved(take(halves, 0, 1 - c), lambda z, x, y, c: (z, x, y, 1 - c))
        mine = mine + moved(mine, lambda z, x, y, c: (z, x, 1 - y, c))
        other = moved(mine, lambda z, x, y, c: (z, x, y, 1 - c))
        return jnp.where(c == 0, jnp.concatenate([mine, other], 0), jnp.concatenate([other, mine], 0))

    def shards(
        token_ids,
        mask_flags,
        time_bins,
        doc_lengths,
        layer_mats,
        mats_first,
        mats_second,
        soap_bases,
        soap_stats,
        vocab_tables,
        tables_first,
        tables_second,
        norm_gains,
        gains_first,
        gains_second,
    ):
        tokens, flags, lengths = token_ids[0], mask_flags[0], doc_lengths[0]
        work_mats = layer_mats.astype(bf16).transpose(0, 2, 1)
        work_tables = vocab_tables.astype(bf16)
        spots = jnp.arange(ROW, dtype=jnp.int32)

        ids = jnp.where(flags == 1, V - 1, tokens)
        owner = ids // per
        same_id = ids[:, None] == ids[None, :]
        before = spots[None, :] < spots[:, None]
        is_first = ~jnp.any(same_id & before, axis=1)
        place = jnp.sum(
            (before & is_first[None, :] & (owner[:, None] == owner[None, :])).astype(jnp.int32), axis=1
        )
        place = jnp.sum(jnp.where(same_id & is_first[None, :], place[None, :], 0), axis=1)
        mats_0 = lax.all_gather(work_mats[0], OWNERS, axis=0, tiled=True)
        slot_ids = jnp.arange(slots_all, dtype=jnp.int32)
        row_ids = jnp.arange(per, dtype=jnp.int32)

        def plan(turn_at):
            at = place - turn_at * CAP
            slot = jnp.where((at >= 0) & (at < CAP), owner * CAP + at, -1)
            hit = slot[:, None] == slot_ids[None, :]
            asked = jnp.max(jnp.where(hit, ids[:, None] % per, -1), axis=0).reshape(n_dev, CAP)
            most = jnp.broadcast_to(jnp.max(place), (n_dev, 128 - CAP))
            asked = jnp.concatenate([asked, most], axis=1)
            asked = lax.all_to_all(asked, OWNERS, 0, 0, tiled=True)
            rows = asked[:, :CAP].reshape(-1)[:, None] == row_ids[None, :]
            return hit, rows, jnp.max(asked[:, CAP]) // CAP + 1

        def fetch(hit, rows):
            sent = nn(rows.astype(bf16), work_tables[0]).astype(bf16)
            got = lax.all_to_all(sent, OWNERS, 0, 0, tiled=True)
            return nn(hit.astype(bf16), got)

        def embed_send(hit, grad):
            return tn(hit.astype(f32), grad, high)

        def exchange(sent):
            return lax.all_to_all(sent, OWNERS, 0, 0, tiled=True)

        def embed_sum(rows, got):
            return tn(rows.astype(f32), got, high)

        def fetch_more(turn_at, residual):
            hit, rows, _ = plan(turn_at)
            return residual + fetch(hit, rows)

        def give_more(turn_at, carry):
            total, grad = carry
            hit, rows, _ = plan(turn_at)
            return total + embed_sum(rows, exchange(embed_send(hit, grad))), grad

        hit_0, rows_0, rounds = plan(0)
        residual = fetch(hit_0, rows_0)
        residual = lax.fori_loop(1, rounds, fetch_more, residual)

        at_fs = lax.axis_index(FS)
        lo = jnp.asarray(kind_lo, jnp.int32)[at_fs]
        hi = jnp.asarray(kind_hi, jnp.int32)[at_fs]
        col_ids = (at_fs * n_dp + lax.axis_index(DP)) * cols + jnp.arange(cols, dtype=jnp.int32)
        kind_ids = sum((col_ids >= b).astype(jnp.int32) for b in BOUNDS[1:-1])
        in_lo = kind_ids == lo

        def stat_scatter(own):
            part = jnp.concatenate(
                [tn(jnp.where(in_lo[:, None], own, 0.0), own, highest), tn(jnp.where(in_lo[:, None], 0.0, own), own, highest)],
                axis=0,
            ).reshape(2, D, D)
            every = jnp.stack(
                [jnp.where(lo == kind, part[0], jnp.where(hi == kind, part[1], 0.0)) for kind in range(KINDS)]
            ).reshape(KINDS * D, D)
            return lax.psum_scatter(every, DATA, scatter_dimension=0, tiled=True)

        ends = jnp.cumsum(lengths)
        passed = spots[:, None] >= ends[None, :]
        doc = jnp.sum(passed.astype(jnp.int32), axis=1)
        position = spots - jnp.sum(jnp.where(passed, lengths[None, :], 0), axis=1)
        tables = pair_tables(position)
        docs = (doc[None, :], jnp.broadcast_to(doc[:, None], (ROW, 128)))

        count = jnp.sum(flags)
        order = jnp.where(flags == 1, jnp.cumsum(flags) - 1, count + jnp.cumsum(1 - flags) - 1)
        at_slot = order[None, :] == jnp.arange(SLOTS, dtype=jnp.int32)[:, None]
        pick = at_slot.astype(bf16)

        def picked(vector):
            return jnp.sum(jnp.where(at_slot, vector[None, :], jnp.zeros((), vector.dtype)), axis=1)

        targets = picked(tokens)
        valid = jnp.arange(SLOTS, dtype=jnp.int32) < count
        code = jnp.where(valid, time_bins[0] + 1, 0)
        slots = (pick, picked(doc)[None, :], pair_tables(picked(position)))

        group_codes = lax.all_gather(jnp.stack([targets, code]), HEAD_GROUP, axis=1, tiled=True)
        residual, group_codes = lax.optimization_barrier((residual, group_codes))
        group_targets, group_codes = group_codes[0], group_codes[1]

        mats_1 = lax.all_gather(work_mats[1], OWNERS, axis=0, tiled=True)
        residual, saved_0 = layer_forward(residual, None, mats_0, norm_gains[0:2], docs, tables)
        if paired:
            x = lax.axis_index("x")
            other = moved(work_tables[1], lambda z, x, y, c: (z, 1 - x, y, c))
            residual, other = lax.optimization_barrier((residual, other))
            head = jnp.concatenate([jnp.where(x == 0, work_tables[1], other), jnp.where(x == 0, other, work_tables[1])], 0)
        else:
            head = lax.all_gather(work_tables[1], "x", axis=0, tiled=True)
        final, saved_1 = layer_forward(residual, slots, mats_1, norm_gains[2:4], docs, tables)

        chosen_full, pull_final = jax.vjp(rms_scale, final, norm_gains[2 * LAYERS])
        states = lax.all_gather(chosen_full.astype(bf16), HEAD_GROUP, axis=0, tiled=True)
        logits = nt(states, head)
        base_shard = lax.axis_index(FS) * n_dp + lax.axis_index("z") * n_x
        vocab_ids = base_shard * per + jnp.arange(n_x * per, dtype=jnp.int32)
        onehot = vocab_ids[None, :] == group_targets[:, None]
        top = jnp.max(logits, axis=1)
        total = jnp.sum(jnp.exp(logits - top[:, None]), axis=1)
        hit_logit = jnp.sum(jnp.where(onehot, logits, 0.0), axis=1)
        parts = jnp.stack([top, total, hit_logit])
        for axes in (FS, "z"):
            each = lax.all_gather(parts, axes, axis=0)
            top = jnp.max(each[:, 0], axis=0)
            parts = jnp.stack(
                [top, jnp.sum(each[:, 1] * jnp.exp(each[:, 0] - top), axis=0), jnp.sum(each[:, 2], axis=0)]
            )
        log_total, target_logit = parts[0] + jnp.log(parts[1]), parts[2]
        weight = jnp.where(group_codes > 0, BINS / jnp.maximum(group_codes, 1).astype(f32), 0.0)
        own_start = lax.axis_index(HEAD_GROUP) * SLOTS
        loss_part = jnp.sum(
            lax.dynamic_slice_in_dim(weight * (log_total - target_logit), own_start, SLOTS)
        )
        grad_logits = (
            weight[:, None] * (jnp.exp(logits - log_total[:, None]) - onehot.astype(f32))
        ).astype(bf16)
        grad_states = lax.psum_scatter(nn(grad_logits, head), HEAD_GROUP, scatter_dimension=0, tiled=True)
        head_part = tn(grad_logits, states)
        grad_states, head_part = lax.optimization_barrier((grad_states, head_part))
        if paired:
            head_part = head_part.reshape(n_x, per, D)
            head_sent = moved(take(head_part, 0, 1 - x), lambda z, x, y, c: (z, 1 - x, y, c))
        else:
            grad_head = lax.psum_scatter(head_part, "x", scatter_dimension=0, tiled=True)
        grad_final, grad_final_gain = pull_final(grad_states)

        cut = WIDE // 2 - 4 * D

        def same(value):
            return value

        middle_1, branch, out_1, gu_1, down_1, gain_f1 = ffn_back(
            grad_final, saved_1, mats_1, norm_gains[2:4], cut, same
        )
        grad_1, qkv_1, gain_a1 = attention_back(
            middle_1, branch, saved_1, slots, mats_1, norm_gains[2:4], docs, tables, same, same
        )
        all_1 = jnp.concatenate([qkv_1, out_1, *gu_1, down_1], axis=0)
        if paired:
            blocks = (n_z, n_x, cols, D)
            lane_1 = Lane(sum_all(all_1.reshape((n_y, n_c) + blocks)))
            grad_1, head_sent = lax.optimization_barrier((grad_1, head_sent))
            grad_head = take(head_part, 0, x) + head_sent
            grad_1 = start(grad_1, lane_1)
            middle_0, branch, out_0, gu_0, down_0, gain_f0 = ffn_back(
                grad_1, saved_0, mats_0, norm_gains[0:2], cut, lambda v: tick(v, lane_1)
            )
            early = jnp.concatenate([gu_0[1], down_0], axis=0)
            middle_0, branch, early = lax.optimization_barrier((middle_0, branch, early))
            early = lax.psum_scatter(early, work_axes, scatter_dimension=0, tiled=True)
            grad_0, qkv_0, gain_a0 = attention_back(
                middle_0, branch, saved_0, None, mats_0, norm_gains[0:2], docs, tables,
                same, lambda v: tick(v, lane_1),
            )
            late = jnp.concatenate([qkv_0, out_0, gu_0[0]], axis=0)
            grad_0, late, early = lax.optimization_barrier((grad_0, late, early))
            late = lax.psum_scatter(late, work_axes, scatter_dimension=0, tiled=True)
            sent = embed_send(hit_0, grad_0)
            sent = tick(sent, lane_1)
            embed_got = exchange(sent)
            tick((), lane_1)
            embed_got = tick(embed_got, lane_1)
            while not lane_1.done:
                tick((), lane_1)
            own_1 = lane_1.result
            work_1 = to_work(own_1)
            work_1, late = lax.optimization_barrier((work_1, late))
            work_0 = jnp.concatenate([late, early], axis=0)
            own_0 = from_work(work_0)
        else:
            own_1 = lax.psum_scatter(all_1, OWNERS, scatter_dimension=0, tiled=True)
            middle_0, branch, out_0, gu_0, down_0, gain_f0 = ffn_back(
                grad_1, saved_0, mats_0, norm_gains[0:2], cut, same
            )
            grad_0, qkv_0, gain_a0 = attention_back(
                middle_0, branch, saved_0, None, mats_0, norm_gains[0:2], docs, tables, same, same
            )
            all_0 = jnp.concatenate([qkv_0, out_0, *gu_0, down_0], axis=0)
            own_0 = lax.psum_scatter(all_0, OWNERS, scatter_dimension=0, tiled=True)
            embed_got, stat_1 = exchange(embed_send(hit_0, grad_0)), stat_scatter(own_1)
            stat_0 = stat_scatter(own_0)
        grad_embed = embed_sum(rows_0, embed_got)
        grad_embed, _ = lax.fori_loop(1, rounds, give_more, (grad_embed, grad_0))

        gain_part = jnp.stack([gain_a0, gain_f0, gain_a1, gain_f1, grad_final_gain])
        own_mats = jnp.stack([own_0, own_1])
        square = jnp.sum(own_mats * own_mats) + jnp.sum(grad_embed * grad_embed) + jnp.sum(grad_head * grad_head)
        scalars = jnp.stack([square, loss_part, count.astype(f32)])
        small = jnp.concatenate([gain_part, jnp.broadcast_to(scalars[:, None], (3, D))], axis=0)
        small = jnp.sum(lax.all_gather(small, ("x", "y", "c"), axis=0), axis=0)
        small = jnp.sum(lax.all_gather(small, "z", axis=0), axis=0)
        gain_sum = small[: 2 * LAYERS + 1]
        square_sum, loss_sum, mask_count = (small[2 * LAYERS + 1 + i, 0] for i in range(3))
        clip_norm = jnp.sqrt(square_sum + jnp.sum(gain_sum * gain_sum)) / mask_count
        factor = jnp.minimum(1.0, clip_limit / clip_norm) / mask_count

        at_dp = lax.axis_index(DP)
        stat_scale = (1.0 - stat_decay) * (factor * factor)
        own_mat = at_dp * n_mats // n_dp
        linear = at_dp * n_fs + at_fs
        basis_start = (linear % sharing) * basis_rows
        flat_stats = soap_stats.reshape(n_mats, D, D)
        if paired:
            y, c = lax.axis_index("y"), lax.axis_index("c")
            starts = ((jnp.arange(2) * 2 + y) * n_dp + at_dp) * cols + c * half
            work_cols = (starts[:, None] + jnp.arange(half)[None, :]).reshape(-1)
            work_kinds = sum((work_cols >= b).astype(jnp.int32) for b in BOUNDS[1:-1])
            to_owner = []
            for work in (work_0, work_1):
                for kind in range(KINDS):
                    mine = jnp.where((work_kinds == kind)[:, None], work, 0.0)
                    to_owner.append(mine[:half] + mine[half:] if merges[kind] else mine)
            most_rows = max(piece.shape[0] for piece in to_owner)
            to_owner = [jnp.pad(piece, ((0, most_rows - piece.shape[0]), (0, 0))) for piece in to_owner]
            columns = lax.all_to_all(jnp.stack(to_owner), DP, 0, 0, tiled=True)
            own_sum = share_stat(columns.reshape(-1, D))
        else:
            own_sum = jnp.concatenate(
                [lax.all_gather(part, DATA, axis=0, tiled=True) for part in (stat_0, stat_1)], axis=0
            ).reshape(n_mats, D, D)[own_mat]
        sum_part = lax.dynamic_slice_in_dim(own_sum, basis_start, basis_rows)
        stat_sums = lax.all_gather(sum_part, DATA, axis=0, tiled=True).reshape(n_mats, D, D)
        own_stat = stat_decay * flat_stats[own_mat] + stat_scale * own_sum
        own_basis = soap_bases.reshape(n_mats, D, D)[own_mat]
        product = nn(own_stat, own_basis, highest)
        gram = tn(product, product, highest)
        rows = lax.dynamic_slice_in_dim(product, basis_start, basis_rows)
        rows, gram, stat_sums = lax.optimization_barrier((rows, gram, stat_sums))
        first, rest = orthogonal_rows(gram, rows, D // (2 * STEPS))
        first, rows, gram = lax.optimization_barrier((first[:, : D // 2], first[:, D // 2 :], rest[D // 2 :, D // 2 :]))
        first = lax.all_gather(first, DATA, axis=0, tiled=True)
        second, _ = orthogonal_rows(gram, rows, D // (2 * STEPS))
        first, second = lax.optimization_barrier((first, second))
        second = lax.all_gather(second, DATA, axis=0, tiled=True)
        new_stats = (stat_decay * flat_stats + stat_scale * stat_sums).reshape(soap_stats.shape)
        new_bases = jnp.concatenate([first, second], axis=1).reshape(soap_bases.shape)

        clipped = own_mats * factor
        basis_lo = jnp.take(soap_bases, lo, axis=1)
        basis_hi = jnp.take(soap_bases, hi, axis=1)

        def by_kind(form, value):
            first = jnp.einsum(form, basis_lo, value, precision=highest)
            second = jnp.einsum(form, basis_hi, value, precision=highest)
            return jnp.where(in_lo[None, None, :], first, second)

        turned = by_kind("lij,lci->ljc", clipped)
        new_mats_first = beta_one * mats_first + (1.0 - beta_one) * turned
        new_mats_second = beta_two * mats_second + (1.0 - beta_two) * turned * turned
        heading = (
            new_mats_first
            / (1.0 - beta_one**STEP)
            / (jnp.sqrt(new_mats_second / (1.0 - beta_two**STEP)) + eps_adam)
        )
        direction = by_kind("lij,ljc->lic", heading)
        new_mats = layer_mats - learn_rate * (direction + decay_weight * layer_mats)
        new_tables, new_tables_first, new_tables_second = adam_update(
            vocab_tables, jnp.stack([grad_embed, grad_head]) * factor, tables_first, tables_second
        )
        new_gains, new_gains_first, new_gains_second = adam_update(
            norm_gains, gain_sum * factor, gains_first, gains_second
        )
        return (
            loss_sum,
            mask_count,
            clip_norm,
            new_mats,
            new_mats_first,
            new_mats_second,
            new_bases,
            new_stats,
            new_tables,
            new_tables_first,
            new_tables_second,
            new_gains,
            new_gains_first,
            new_gains_second,
        )

    return shards


def solution(mesh):
    n_dp, n_fs = mesh.shape["dp"], mesh.shape["fsdp"]
    n_x = 2 ** ((n_dp.bit_length() - 1) // 2)
    fine = Mesh(mesh.devices.reshape(n_dp // n_x, n_x, n_fs // 2, 2), ("z", "x", "y", "c"))
    rows, row = P(DATA, None), P(DATA)
    mats, tables = P(None, None, OWNERS), P(None, OWNERS, None)
    return jax.shard_map(
        make_shards(dict(fine.shape)),
        mesh=fine,
        in_specs=(rows, rows, row, rows, mats, mats, mats, P(), P(), tables, tables, tables, P(), P(), P()),
        out_specs=(P(), P(), P(), mats, mats, mats, P(), P(), tables, tables, tables, P(), P(), P()),
        check_vma=False,
    )
```

```python
import jax
import jax.numpy as jnp
import numpy as np
from jax import lax
from jax.experimental import pallas as pl
from jax.experimental.pallas import tpu as pltpu
from jax.sharding import Mesh
from jax.sharding import PartitionSpec as P

D = 768
HEADS = 12
HD = 64
FF = 2048
V = 32000
LAYERS = 2
ROW = 1024
SLOTS = 256
BINS = 8
STEP = 10
WIDE = 9216
KINDS = 4
BOUNDS = (0, 3 * D, 4 * D, 4 * D + 2 * FF, WIDE)
CAP = 40
PAIR = 2 * HD
PAIRS = D // PAIR
BLOCK = 256
VMEM_CAP = 56 * 2**20
STEPS = 128
LIGHT = pl.CostEstimate(flops=1000, bytes_accessed=1000, transcendentals=0)
TILE = 8

bf16 = jnp.bfloat16
f32 = jnp.float32
highest = lax.Precision.HIGHEST
high = lax.Precision.HIGH
learn_rate = 0.05
beta_one = 0.9
beta_two = 0.95
eps_adam = 1e-08
decay_weight = 0.1
stat_decay = 0.95
clip_limit = 0.05
norm_eps = 1e-05

OWNERS = ("y", "c", "z", "x")
DATA = ("z", "x", "y", "c")
DP = ("z", "x")
FS = ("y", "c")
HEAD_GROUP = ("z", "y", "c")


def dot(a, b, dims, precision=None):
    return lax.dot_general(a, b, (dims, ((), ())), precision=precision, preferred_element_type=f32)


def nn(a, b, precision=None):
    return dot(a, b, ((1,), (0,)), precision)


def nt(a, b, precision=None):
    return dot(a, b, ((1,), (1,)), precision)


def tn(a, b, precision=None):
    return dot(a, b, ((0,), (0,)), precision)


def rms_scale(values, gain):
    return values * lax.rsqrt(jnp.mean(values * values, axis=-1, keepdims=True) + norm_eps) * gain


def silu_up(gate, up):
    return jax.nn.silu(gate) * up


def mm(a, b, ca, cb):
    return lax.dot_general(a, b, (((ca,), (cb,)), ((), ())), preferred_element_type=f32)


def rotate(x, cosine, sine, low_half):
    other = jnp.where(low_half, pltpu.roll(x, PAIR - HD // 2, 1), pltpu.roll(x, HD // 2, 1))
    return x * cosine + other * sine


def lane_masks():
    lane = lax.broadcasted_iota(jnp.int32, (1, PAIR), 1)
    return lane % HD < HD // 2, (lane < HD, lane >= HD)


def attend_kernel(q_ref, k_ref, v_ref, cq_ref, sq_ref, ck_ref, sk_ref, docq_ref, dock_ref,
                  out_ref, qs_ref, kt_ref, vb_ref, lse_ref):
    low_half, own = lane_masks()
    queries = rotate(q_ref[...], cq_ref[...], sq_ref[...], low_half).astype(bf16)
    qs_ref[...] = queries * jnp.asarray(HD ** (-0.5), bf16)
    keys = rotate(k_ref[...], ck_ref[...], sk_ref[...], low_half).astype(bf16)
    kt_ref[...] = keys
    values = v_ref[...]
    vb_ref[...] = values.astype(bf16)
    values_t = values.T.astype(bf16)
    dock = jnp.concatenate([dock_ref[...]] * (BLOCK // 128), axis=1)
    for at in range(0, q_ref.shape[0], BLOCK):
        rows = slice(at, at + BLOCK)
        same = dock == docq_ref[:, rows]
        outs = []
        for h in range(2):
            scores = mm(jnp.where(own[h], keys, 0), qs_ref[rows, :], 1, 1)
            scores = jnp.where(same, scores, -1000000000.0)
            top = jnp.max(scores, axis=0, keepdims=True)
            soft = jnp.exp(scores - top)
            total = jnp.sum(soft, axis=0, keepdims=True)
            lse_ref[0, h : h + 1, rows] = top + jnp.log(total)
            soft = (soft * (1.0 / total)).astype(bf16)
            outs.append(mm(values_t[h * HD : (h + 1) * HD], soft, 1, 0))
        out_ref[rows, :] = jnp.concatenate(outs, axis=0).T.astype(bf16)


def attend_back_kernel(qs_ref, k_ref, v_ref, g_ref, lse_ref, cq_ref, sq_ref, ck_ref, sk_ref, docq_ref, dock_ref,
                       dq_ref, dk_ref, dv_ref, dk_sum, dv_sum):
    low_half, own = lane_masks()
    keys, values = k_ref[...], v_ref[...]
    keys_t = keys.astype(f32).T.astype(bf16)
    dock = jnp.concatenate([dock_ref[...]] * (BLOCK // 128), axis=1)
    for at in range(0, qs_ref.shape[0], BLOCK):
        rows = slice(at, at + BLOCK)
        same = dock == docq_ref[:, rows]
        queries, grad = qs_ref[rows, :], g_ref[rows, :]
        back = []
        for h in range(2):
            scores = mm(jnp.where(own[h], keys, 0), queries, 1, 1)
            soft = jnp.exp(jnp.where(same, scores, -1000000000.0) - lse_ref[0, h : h + 1, rows])
            grad_soft = mm(jnp.where(own[h], values, 0), grad, 1, 1)
            delta = jnp.sum(soft * grad_soft, axis=0, keepdims=True)
            grad_scores = (soft * (grad_soft - delta)).astype(bf16)
            dv = mm(soft.astype(bf16), jnp.where(own[h], grad, 0), 1, 0)
            dk = mm(grad_scores, jnp.where(own[h], queries, 0), 1, 0)
            if at == 0 and h == 0:
                dv_sum[...] = dv
                dk_sum[...] = dk
            else:
                dv_sum[...] += dv
                dk_sum[...] += dk
            back.append(mm(keys_t[h * HD : (h + 1) * HD], grad_scores, 1, 0))
        dq = jnp.concatenate(back, axis=0).T * HD ** (-0.5)
        dq_ref[rows, :] = rotate(dq, cq_ref[rows, :], -sq_ref[rows, :], low_half).astype(bf16)
    dk_ref[...] = rotate(dk_sum[...], ck_ref[...], -sk_ref[...], low_half).astype(bf16)
    dv_ref[...] = dv_sum[...].astype(bf16)


def column(rows, shift=0):
    return pl.BlockSpec((rows, PAIR), lambda h: (0, h + shift))


def whole(shape):
    return pl.BlockSpec(shape, lambda h: (0,) * len(shape))


def stat_spec(rows):
    return pl.BlockSpec((1, 2, rows), lambda h: (h, 0, 0))


def attend(q, kv, turn_q, turn_k, doc_q, doc_k):
    n_q, n_k = q.shape[0], kv.shape[0]
    low = jax.ShapeDtypeStruct((n_q, D), bf16)
    low_k = jax.ShapeDtypeStruct((n_k, D), bf16)
    return pl.pallas_call(
        attend_kernel,
        grid=(PAIRS,),
        in_specs=[column(n_q), column(n_k), column(n_k, PAIRS)]
        + [whole((n_q, PAIR))] * 2 + [whole((n_k, PAIR))] * 2 + [whole((1, n_q)), whole((n_k, 128))],
        out_specs=[column(n_q), column(n_q), column(n_k), column(n_k), stat_spec(n_q)],
        out_shape=[low, low, low_k, low_k, jax.ShapeDtypeStruct((PAIRS, 2, n_q), f32)],
        compiler_params=pltpu.CompilerParams(vmem_limit_bytes=VMEM_CAP),
        cost_estimate=LIGHT,
        name="attend",
    )(q, kv, kv, *turn_q, *turn_k, doc_q, doc_k)


def attend_back(qs, k, v, grad, lse, turn_q, turn_k, doc_q, doc_k):
    n_q, n_k = qs.shape[0], k.shape[0]
    low = jax.ShapeDtypeStruct((n_q, D), bf16)
    low_k = jax.ShapeDtypeStruct((n_k, D), bf16)
    return pl.pallas_call(
        attend_back_kernel,
        grid=(PAIRS,),
        in_specs=[column(n_q), column(n_k), column(n_k), column(n_q), stat_spec(n_q)]
        + [whole((n_q, PAIR))] * 2 + [whole((n_k, PAIR))] * 2 + [whole((1, n_q)), whole((n_k, 128))],
        out_specs=[column(n_q), column(n_k), column(n_k)],
        out_shape=[low, low_k, low_k],
        scratch_shapes=[pltpu.VMEM((n_k, PAIR), f32)] * 2,
        compiler_params=pltpu.CompilerParams(vmem_limit_bytes=VMEM_CAP),
        cost_estimate=LIGHT,
        name="attend_back",
    )(qs, k, v, grad, lse, *turn_q, *turn_k, doc_q, doc_k)


def pair_tables(position):
    half = HD // 2
    frequency = 10000.0 ** (-jnp.arange(half, dtype=f32) / half)
    angles = position[:, None].astype(f32) * frequency
    cosine, sine = jnp.cos(angles), jnp.sin(angles)
    return jnp.concatenate([cosine] * 4, axis=1), jnp.concatenate([-sine, sine] * 2, axis=1)


def fm(a, b, ca, cb):
    return lax.dot_general(a, b, (((ca,), (cb,)), ((), ())), precision=highest, preferred_element_type=f32)


def inverse_factor(block):
    row_at = lax.broadcasted_iota(jnp.int32, (STEPS, STEPS), 0)
    col_at = lax.broadcasted_iota(jnp.int32, (STEPS, STEPS), 1)
    eye = jnp.where(row_at == col_at, 1.0, 0.0).astype(f32)
    sub = lax.broadcasted_iota(jnp.int32, (TILE, 1), 0)
    n = STEPS // TILE
    left = [block[i * TILE : (i + 1) * TILE] for i in range(n)]
    right = [eye[i * TILE : (i + 1) * TILE] for i in range(n)]
    for j in range(STEPS):
        at, within = divmod(j, TILE)
        row = left[at][within : within + 1]
        scale = 1.0 / row[:, j : j + 1]
        row = row * scale
        mate = right[at][within : within + 1] * scale
        for i in range(at, n):
            column = left[i][:, j : j + 1]
            if i == at:
                column = jnp.where(sub > within, column, 0.0)
            left[i] = left[i] - column * row
            right[i] = right[i] - column * mate
    upper = jnp.concatenate(left, axis=0)
    pivots = jnp.sum(jnp.where(row_at == col_at, upper, 0.0), axis=1, keepdims=True)
    return jnp.concatenate(right, axis=0) * lax.rsqrt(pivots)


def orthogonal_kernel(gram_ref, rows_ref, out_ref, rest_ref):
    rest_ref[...] = gram_ref[...]
    out_ref[...] = rows_ref[...]
    lane = lax.broadcasted_iota(jnp.int32, (1, D), 1)

    def body(b, _):
        start = pl.multiple_of(b * STEPS, STEPS)
        here = pl.ds(start, STEPS)
        inverse = inverse_factor(rest_ref[here, here])
        upper = jnp.where(lane >= start + STEPS, fm(inverse, rest_ref[here, :], 1, 0), 0.0)
        done = fm(out_ref[:, here], inverse, 1, 1)
        out_ref[...] -= fm(done, upper, 1, 0)
        out_ref[:, here] = done
        rest_ref[...] -= fm(upper, upper, 0, 0)
        return 0

    lax.fori_loop(0, D // STEPS, body, 0)


def orthogonal_rows(gram, rows):
    return pl.pallas_call(
        orthogonal_kernel,
        out_shape=jax.ShapeDtypeStruct(rows.shape, f32),
        in_specs=[pl.BlockSpec(memory_space=pltpu.VMEM)] * 2,
        out_specs=pl.BlockSpec(memory_space=pltpu.VMEM),
        scratch_shapes=[pltpu.VMEM((D, D), f32)],
        compiler_params=pltpu.CompilerParams(vmem_limit_bytes=40 * 2**20),
        cost_estimate=pl.CostEstimate(flops=2 * 10**11, bytes_accessed=8 * D * D, transcendentals=0),
        name="orthogonal_rows",
    )(gram, rows)


def adam_update(weight, grad, first, second):
    first = beta_one * first + (1.0 - beta_one) * grad
    second = beta_two * second + (1.0 - beta_two) * grad * grad
    heading = (
        first / (1.0 - beta_one**STEP) / (jnp.sqrt(second / (1.0 - beta_two**STEP)) + eps_adam)
    )
    return (weight - learn_rate * (heading + decay_weight * weight), first, second)


def parts_of(weights):
    return (
        weights[: 3 * D],
        weights[3 * D : 4 * D],
        weights[4 * D : 4 * D + 2 * FF],
        weights[4 * D + 2 * FF :],
    )


def layer_forward(residual, slots, weights, gains, doc, tables):
    w_qkv, w_out, w_gu, w_down = parts_of(weights)
    normed = rms_scale(residual, gains[0]).astype(bf16)
    if slots is None:
        rows_in, normed_q, doc_q, tables_q = residual, normed, doc[0], tables
    else:
        pick, doc_q, tables_q = slots
        rows_in = nn(pick.astype(f32), residual, highest)
        normed_q = nn(pick, normed).astype(bf16)
    attended, *kept = attend(
        nt(normed_q, w_qkv[:D]), nt(normed, w_qkv[D:]), tables_q, tables, doc_q, doc[1]
    )
    middle = rows_in + nt(attended, w_out)
    normed_ffn = rms_scale(middle, gains[1]).astype(bf16)
    gate_up = nt(normed_ffn, w_gu)
    activated = silu_up(gate_up[:, :FF], gate_up[:, FF:]).astype(bf16)
    result = middle + nn(activated, w_down)
    saved = (residual, normed, normed_q, kept, attended, middle, normed_ffn, gate_up, activated)
    return result, saved


def ffn_back(grad_out, saved, weights, gains, cut, between):
    _, _, w_gu, w_down = parts_of(weights)
    _, _, _, _, attended, middle, normed_ffn, gate_up, activated = saved
    grad_low = grad_out.astype(bf16)
    grad_down = tn(activated, grad_low)
    grad_act = nt(grad_low, w_down)
    _, pull_act = jax.vjp(silu_up, gate_up[:, :FF], gate_up[:, FF:])
    grad_gate_up = jnp.concatenate(pull_act(grad_act), axis=1).astype(bf16)
    grad_gate_up, grad_down = between((grad_gate_up, grad_down))
    grad_gu = [tn(grad_gate_up[:, :cut], normed_ffn), tn(grad_gate_up[:, cut:], normed_ffn)]
    _, pull_ffn = jax.vjp(rms_scale, middle, gains[1])
    grad_middle, grad_gain = pull_ffn(nn(grad_gate_up, w_gu))
    grad_middle = grad_out + grad_middle
    branch = grad_middle.astype(bf16)
    return grad_middle, branch, tn(branch, attended), grad_gu, grad_down, grad_gain


def attention_back(grad_middle, branch, saved, slots, weights, gains, doc, tables, before, between):
    w_qkv, w_out, _, _ = parts_of(weights)
    residual, normed, normed_q, kept, _, _, _, _, _ = saved
    grad_att = before(nn(branch, w_out).astype(bf16))
    if slots is None:
        doc_q, tables_q = doc[0], tables
    else:
        pick, doc_q, tables_q = slots
    qs, k, v, lse = kept
    grads = attend_back(qs, k, v, grad_att, lse, tables_q, tables, doc_q, doc[1])
    grad_q, grad_k, grad_v = between(grads)
    grad_qkv = jnp.concatenate([tn(grad_q, normed_q), tn(grad_k, normed), tn(grad_v, normed)], 0)
    grad_in = nn(grad_k, w_qkv[D : 2 * D]) + nn(grad_v, w_qkv[2 * D :])
    grad_in_q = nn(grad_q, w_qkv[:D])
    if slots is not None:
        grad_in_q = tn(pick.astype(f32), grad_in_q, highest)
        grad_middle = tn(pick.astype(f32), grad_middle, highest)
    _, pull_att = jax.vjp(rms_scale, residual, gains[0])
    grad_residual, grad_gain = pull_att(grad_in + grad_in_q)
    return grad_middle + grad_residual, grad_qkv, grad_gain


def make_shards(sizes):
    n_z, n_x, n_y, n_c = (sizes[a] for a in ("z", "x", "y", "c"))
    n_dp, n_fs = n_z * n_x, n_y * n_c
    n_dev = n_dp * n_fs
    per = V // n_dev
    cols = WIDE // n_dev
    span = WIDE // n_fs
    n_mats = LAYERS * KINDS
    stat_rows = D // n_dp
    sharing = n_dev // n_mats
    basis_rows = D // sharing
    kind_of = np.searchsorted(np.array(BOUNDS[1:]), np.arange(WIDE), side="right")
    kind_lo = [int(kind_of[f * span]) for f in range(n_fs)]
    kind_hi = [int(kind_of[(f + 1) * span - 1]) for f in range(n_fs)]
    slots_all = n_dev * CAP
    shape = (n_z, n_x, n_y, n_c)
    paired = n_x == 2 and n_y == 2 and n_c == 2 and n_dp == n_mats

    def moved(value, target):
        pairs = []
        for source in np.ndindex(n_z, n_x, n_y, n_c):
            dest = target(*source)
            if dest is not None:
                pairs.append((np.ravel_multi_index(source, shape), np.ravel_multi_index(dest, shape)))
        return lax.ppermute(value, DATA, [(int(s), int(d)) for s, d in pairs])

    def take(value, axis, at):
        return lax.dynamic_index_in_dim(value, at, axis, keepdims=False)

    def z_line(value, inside):
        at = lax.axis_index("z")
        up, down = 0.0, 0.0
        for k in range(n_z - 1, 0, -1):
            up = value[jnp.minimum(at + k, n_z - 1)] + up
            down = value[jnp.maximum(at - k, 0)] + down
            up, down = yield (
                (up, lambda z, x, y, c: (z + 1, x, y, c) if inside(y, c) and z + k < n_z else None),
                (down, lambda z, x, y, c: (z - 1, x, y, c) if inside(y, c) and z >= k else None),
            )
        return value[at] + up + down

    def sum_all(value):
        c, y, x = lax.axis_index("c"), lax.axis_index("y"), lax.axis_index("x")
        rows = value.shape[-2] // 2

        def by_x(z, x, y, c):
            return z, 1 - x, y, c

        def by_y(z, x, y, c):
            return z, x, 1 - y, c

        kept = take(value, 1, c)
        (sent,) = yield ((take(value, 1, 1 - c), lambda z, x, y, c: (z, x, y, 1 - c)),)
        first = kept[..., :rows, :] + sent[..., :rows, :]
        second = kept[..., rows:, :] + sent[..., rows:, :]
        sent_x, sent_y = yield ((take(first, 2, 1 - x), by_x), (take(second, 0, 1 - y), by_y))
        first, second = take(first, 2, x) + sent_x, take(second, 0, y) + sent_y
        sent_y, sent_x = yield ((take(first, 0, 1 - y), by_y), (take(second, 1, 1 - x), by_x))
        first, second = take(first, 0, y) + sent_y, take(second, 1, x) + sent_x
        return (yield from z_line(jnp.concatenate([first, second], axis=-2), lambda y, c: True))

    class Lane:
        def __init__(self, steps):
            self.steps, self.done, self.flying = steps, False, []
            self.asks = next(steps)

        def land(self, landed):
            try:
                self.asks = self.steps.send(landed)
            except StopIteration as end:
                self.done, self.result = True, end.value

    def start(value, *lanes):
        lanes = [lane for lane in lanes if not lane.done]
        operands = [[operand for operand, _ in lane.asks] for lane in lanes]
        value, operands = lax.optimization_barrier((value, operands))
        for lane, each in zip(lanes, operands):
            lane.flying = [moved(operand, target) for operand, (_, target) in zip(each, lane.asks)]
        return value

    def tick(value, *lanes):
        lanes = [lane for lane in lanes if not lane.done]
        value, landed = lax.optimization_barrier((value, [lane.flying for lane in lanes]))
        for lane, each in zip(lanes, landed):
            lane.land(each)
        return start(value, *lanes)

    half = cols // 2
    has = [[(kind_of.reshape(n_fs, n_dp, cols) == kind)[f].any(axis=1) for f in range(n_fs)] for kind in range(KINDS)]
    merges = [n_fs == 4 and not any((has[k][y] & has[k][2 + y]).any() for y in range(2)) for k in range(KINDS)]
    work_axes = ("y", "z", "x", "c")

    def to_work(own):
        y, c = lax.axis_index("y"), lax.axis_index("c")
        pieces = own.reshape(1, 2, half, D) * (jnp.arange(2)[:, None, None, None] == c)
        got = lax.all_to_all(pieces.reshape(-1, D), FS, 0, 0, tiled=True).reshape(2, 2, half, D)
        return take(got, 1, y).reshape(-1, D)

    def from_work(work):
        y, c = lax.axis_index("y"), lax.axis_index("c")
        pieces = work.reshape(2, 1, half, D) * (jnp.arange(2)[None, :, None, None] == y)
        got = lax.all_to_all(pieces.reshape(-1, D), FS, 0, 0, tiled=True).reshape(2, 2, half, D)
        return take(got, 0, c).reshape(-1, D)

    def share_stat(columns):
        part = tn(columns, columns, highest)
        c = lax.axis_index("c")
        halves = part.reshape(2, D // 2, D)
        mine = take(halves, 0, c) + moved(take(halves, 0, 1 - c), lambda z, x, y, c: (z, x, y, 1 - c))
        mine = mine + moved(mine, lambda z, x, y, c: (z, x, 1 - y, c))
        other = moved(mine, lambda z, x, y, c: (z, x, y, 1 - c))
        return jnp.where(c == 0, jnp.concatenate([mine, other], 0), jnp.concatenate([other, mine], 0))

    def shards(
        token_ids,
        mask_flags,
        time_bins,
        doc_lengths,
        layer_mats,
        mats_first,
        mats_second,
        soap_bases,
        soap_stats,
        vocab_tables,
        tables_first,
        tables_second,
        norm_gains,
        gains_first,
        gains_second,
    ):
        tokens, flags, lengths = token_ids[0], mask_flags[0], doc_lengths[0]
        work_mats = layer_mats.astype(bf16).transpose(0, 2, 1)
        work_tables = vocab_tables.astype(bf16)
        spots = jnp.arange(ROW, dtype=jnp.int32)

        ids = jnp.where(flags == 1, V - 1, tokens)
        owner = ids // per
        same_id = ids[:, None] == ids[None, :]
        before = spots[None, :] < spots[:, None]
        is_first = ~jnp.any(same_id & before, axis=1)
        place = jnp.sum(
            (before & is_first[None, :] & (owner[:, None] == owner[None, :])).astype(jnp.int32), axis=1
        )
        place = jnp.sum(jnp.where(same_id & is_first[None, :], place[None, :], 0), axis=1)
        mats_0 = lax.all_gather(work_mats[0], OWNERS, axis=0, tiled=True)
        slot_ids = jnp.arange(slots_all, dtype=jnp.int32)
        row_ids = jnp.arange(per, dtype=jnp.int32)

        def plan(turn_at):
            at = place - turn_at * CAP
            slot = jnp.where((at >= 0) & (at < CAP), owner * CAP + at, -1)
            hit = slot[:, None] == slot_ids[None, :]
            asked = jnp.max(jnp.where(hit, ids[:, None] % per, -1), axis=0).reshape(n_dev, CAP)
            most = jnp.broadcast_to(jnp.max(place), (n_dev, 128 - CAP))
            asked = jnp.concatenate([asked, most], axis=1)
            asked = lax.all_to_all(asked, OWNERS, 0, 0, tiled=True)
            rows = asked[:, :CAP].reshape(-1)[:, None] == row_ids[None, :]
            return hit, rows, jnp.max(asked[:, CAP]) // CAP + 1

        def fetch(hit, rows):
            sent = nn(rows.astype(bf16), work_tables[0]).astype(bf16)
            got = lax.all_to_all(sent, OWNERS, 0, 0, tiled=True)
            return nn(hit.astype(bf16), got)

        def embed_send(hit, grad):
            return tn(hit.astype(f32), grad, high)

        def exchange(sent):
            return lax.all_to_all(sent, OWNERS, 0, 0, tiled=True)

        def embed_sum(rows, got):
            return tn(rows.astype(f32), got, high)

        def fetch_more(turn_at, residual):
            hit, rows, _ = plan(turn_at)
            return residual + fetch(hit, rows)

        def give_more(turn_at, carry):
            total, grad = carry
            hit, rows, _ = plan(turn_at)
            return total + embed_sum(rows, exchange(embed_send(hit, grad))), grad

        hit_0, rows_0, rounds = plan(0)
        residual = fetch(hit_0, rows_0)
        residual = lax.fori_loop(1, rounds, fetch_more, residual)

        at_fs, at_dp = lax.axis_index(FS), lax.axis_index(DP)
        lo = jnp.asarray(kind_lo, jnp.int32)[at_fs]
        hi = jnp.asarray(kind_hi, jnp.int32)[at_fs]
        col_ids = (at_fs * n_dp + lax.axis_index(DP)) * cols + jnp.arange(cols, dtype=jnp.int32)
        kind_ids = sum((col_ids >= b).astype(jnp.int32) for b in BOUNDS[1:-1])
        in_lo = kind_ids == lo

        def stat_scatter(own):
            part = jnp.concatenate(
                [tn(jnp.where(in_lo[:, None], own, 0.0), own, highest), tn(jnp.where(in_lo[:, None], 0.0, own), own, highest)],
                axis=0,
            ).reshape(2, D, D)
            every = jnp.stack(
                [jnp.where(lo == kind, part[0], jnp.where(hi == kind, part[1], 0.0)) for kind in range(KINDS)]
            ).reshape(KINDS * D, D)
            return lax.psum_scatter(every, DATA, scatter_dimension=0, tiled=True)

        ends = jnp.cumsum(lengths)
        passed = spots[:, None] >= ends[None, :]
        doc = jnp.sum(passed.astype(jnp.int32), axis=1)
        position = spots - jnp.sum(jnp.where(passed, lengths[None, :], 0), axis=1)
        tables = pair_tables(position)
        docs = (doc[None, :], jnp.broadcast_to(doc[:, None], (ROW, 128)))

        count = jnp.sum(flags)
        order = jnp.where(flags == 1, jnp.cumsum(flags) - 1, count + jnp.cumsum(1 - flags) - 1)
        at_slot = order[None, :] == jnp.arange(SLOTS, dtype=jnp.int32)[:, None]
        pick = at_slot.astype(bf16)

        def picked(vector):
            return jnp.sum(jnp.where(at_slot, vector[None, :], jnp.zeros((), vector.dtype)), axis=1)

        targets = picked(tokens)
        valid = jnp.arange(SLOTS, dtype=jnp.int32) < count
        code = jnp.where(valid, time_bins[0] + 1, 0)
        slots = (pick, picked(doc)[None, :], pair_tables(picked(position)))

        group_codes = lax.all_gather(jnp.stack([targets, code]), HEAD_GROUP, axis=1, tiled=True)
        residual, group_codes = lax.optimization_barrier((residual, group_codes))
        group_targets, group_codes = group_codes[0], group_codes[1]

        mats_1 = lax.all_gather(work_mats[1], OWNERS, axis=0, tiled=True)
        residual, saved_0 = layer_forward(residual, None, mats_0, norm_gains[0:2], docs, tables)
        if paired:
            x = lax.axis_index("x")
            other = moved(work_tables[1], lambda z, x, y, c: (z, 1 - x, y, c))
            residual, other = lax.optimization_barrier((residual, other))
            head = jnp.concatenate([jnp.where(x == 0, work_tables[1], other), jnp.where(x == 0, other, work_tables[1])], 0)
        else:
            head = lax.all_gather(work_tables[1], "x", axis=0, tiled=True)
        final, saved_1 = layer_forward(residual, slots, mats_1, norm_gains[2:4], docs, tables)

        chosen_full, pull_final = jax.vjp(rms_scale, final, norm_gains[2 * LAYERS])
        states = lax.all_gather(chosen_full.astype(bf16), HEAD_GROUP, axis=0, tiled=True)
        logits = nt(states, head)
        base_shard = lax.axis_index(FS) * n_dp + lax.axis_index("z") * n_x
        vocab_ids = base_shard * per + jnp.arange(n_x * per, dtype=jnp.int32)
        onehot = vocab_ids[None, :] == group_targets[:, None]
        top = jnp.max(logits, axis=1)
        total = jnp.sum(jnp.exp(logits - top[:, None]), axis=1)
        hit_logit = jnp.sum(jnp.where(onehot, logits, 0.0), axis=1)
        parts = jnp.stack([top, total, hit_logit])
        for axes in (FS, "z"):
            each = lax.all_gather(parts, axes, axis=0)
            top = jnp.max(each[:, 0], axis=0)
            parts = jnp.stack(
                [top, jnp.sum(each[:, 1] * jnp.exp(each[:, 0] - top), axis=0), jnp.sum(each[:, 2], axis=0)]
            )
        log_total, target_logit = parts[0] + jnp.log(parts[1]), parts[2]
        weight = jnp.where(group_codes > 0, BINS / jnp.maximum(group_codes, 1).astype(f32), 0.0)
        own_start = lax.axis_index(HEAD_GROUP) * SLOTS
        loss_part = jnp.sum(
            lax.dynamic_slice_in_dim(weight * (log_total - target_logit), own_start, SLOTS)
        )
        grad_logits = (
            weight[:, None] * (jnp.exp(logits - log_total[:, None]) - onehot.astype(f32))
        ).astype(bf16)
        grad_states = lax.psum_scatter(nn(grad_logits, head), HEAD_GROUP, scatter_dimension=0, tiled=True)
        head_part = tn(grad_logits, states)
        grad_states, head_part = lax.optimization_barrier((grad_states, head_part))
        if paired:
            head_part = head_part.reshape(n_x, per, D)
            head_sent = moved(take(head_part, 0, 1 - x), lambda z, x, y, c: (z, 1 - x, y, c))
        else:
            grad_head = lax.psum_scatter(head_part, "x", scatter_dimension=0, tiled=True)
        grad_final, grad_final_gain = pull_final(grad_states)

        cut = WIDE // 2 - 4 * D

        def same(value):
            return value

        def stat_of_owner(work_0, work_1):
            y, c = lax.axis_index("y"), lax.axis_index("c")
            starts = ((jnp.arange(2) * 2 + y) * n_dp + at_dp) * cols + c * half
            work_cols = (starts[:, None] + jnp.arange(half)[None, :]).reshape(-1)
            work_kinds = sum((work_cols >= b).astype(jnp.int32) for b in BOUNDS[1:-1])
            to_owner = []
            for work in (work_0, work_1):
                for kind in range(KINDS):
                    mine = jnp.where((work_kinds == kind)[:, None], work, 0.0)
                    to_owner.append(mine[:half] + mine[half:] if merges[kind] else mine)
            most_rows = max(piece.shape[0] for piece in to_owner)
            to_owner = [jnp.pad(piece, ((0, most_rows - piece.shape[0]), (0, 0))) for piece in to_owner]
            columns = lax.all_to_all(jnp.stack(to_owner), DP, 0, 0, tiled=True)
            return share_stat(columns.reshape(-1, D))

        own_mat = at_dp * n_mats // n_dp
        flat_stats = soap_stats.reshape(n_mats, D, D)
        own_basis = soap_bases.reshape(n_mats, D, D)[own_mat]
        old_product = nn(flat_stats[own_mat], own_basis, highest)

        def rows_sum(rows):
            return lax.psum_scatter(rows, work_axes if paired else OWNERS, scatter_dimension=0, tiled=True)

        middle_1, branch, out_1, gu_1, down_1, gain_f1 = ffn_back(
            grad_final, saved_1, mats_1, norm_gains[2:4], cut, same
        )
        grad_1, qkv_1, gain_a1 = attention_back(
            middle_1, branch, saved_1, slots, mats_1, norm_gains[2:4], docs, tables, same, same
        )
        if paired:
            all_1 = jnp.concatenate([qkv_1, out_1, *gu_1, down_1], axis=0)
            lane_1 = Lane(sum_all(all_1.reshape(n_y, n_c, n_z, n_x, cols, D)))
            grad_1, head_sent = lax.optimization_barrier((grad_1, head_sent))
            grad_head = take(head_part, 0, x) + head_sent
            grad_1 = start(grad_1, lane_1)
            middle_0, branch, out_0, gu_0, down_0, gain_f0 = ffn_back(
                grad_1, saved_0, mats_0, norm_gains[0:2], cut, lambda v: tick(v, lane_1)
            )
            early_0 = jnp.concatenate([gu_0[1], down_0], axis=0)
            middle_0, branch, early_0 = lax.optimization_barrier((middle_0, branch, early_0))
            early_0 = rows_sum(early_0)
            grad_0, qkv_0, gain_a0 = attention_back(
                middle_0, branch, saved_0, None, mats_0, norm_gains[0:2], docs, tables,
                same, lambda v: tick(v, lane_1),
            )
            late_0 = jnp.concatenate([qkv_0, out_0, gu_0[0]], axis=0)
            grad_0, late_0, early_0 = lax.optimization_barrier((grad_0, late_0, early_0))
            late_0 = rows_sum(late_0)
            sent = embed_send(hit_0, grad_0)
            sent = tick(sent, lane_1)
            while not lane_1.done:
                tick((), lane_1)
            own_1 = lane_1.result
            work_1 = to_work(own_1)
            work_1, late_0, sent, old_product = lax.optimization_barrier((work_1, late_0, sent, old_product))
            embed_got = exchange(sent)
            work_0 = jnp.concatenate([late_0, early_0], axis=0)
            own_sum = stat_of_owner(work_0, work_1)
            own_sum, embed_got = lax.optimization_barrier((own_sum, embed_got))
            own_0 = from_work(work_0)
        else:
            own_1 = rows_sum(jnp.concatenate([qkv_1, out_1, *gu_1, down_1], axis=0))
            middle_0, branch, out_0, gu_0, down_0, gain_f0 = ffn_back(
                grad_1, saved_0, mats_0, norm_gains[0:2], cut, same
            )
            grad_0, qkv_0, gain_a0 = attention_back(
                middle_0, branch, saved_0, None, mats_0, norm_gains[0:2], docs, tables, same, same
            )
            own_0 = rows_sum(jnp.concatenate([qkv_0, out_0, *gu_0, down_0], axis=0))
            embed_got = exchange(embed_send(hit_0, grad_0))
            stat_0, stat_1 = stat_scatter(own_0), stat_scatter(own_1)
        grad_embed = embed_sum(rows_0, embed_got)
        grad_embed, _ = lax.fori_loop(1, rounds, give_more, (grad_embed, grad_0))

        gain_part = jnp.stack([gain_a0, gain_f0, gain_a1, gain_f1, grad_final_gain])
        held = jnp.concatenate([work_0, work_1] if paired else [own_0, own_1], axis=0)
        square = jnp.sum(held * held) + jnp.sum(grad_embed * grad_embed) + jnp.sum(grad_head * grad_head)
        scalars = jnp.stack([square, loss_part, count.astype(f32)])
        small = jnp.concatenate([gain_part, jnp.broadcast_to(scalars[:, None], (3, D))], axis=0)
        small = jnp.sum(lax.all_gather(small, ("x", "y", "c"), axis=0), axis=0)
        small = jnp.sum(lax.all_gather(small, "z", axis=0), axis=0)
        gain_sum = small[: 2 * LAYERS + 1]
        square_sum, loss_sum, mask_count = (small[2 * LAYERS + 1 + i, 0] for i in range(3))
        clip_norm = jnp.sqrt(square_sum + jnp.sum(gain_sum * gain_sum)) / mask_count
        factor = jnp.minimum(1.0, clip_limit / clip_norm) / mask_count

        stat_scale = (1.0 - stat_decay) * (factor * factor)
        linear = at_dp * n_fs + at_fs
        basis_start = (linear % sharing) * basis_rows
        if not paired:
            own_sum = jnp.concatenate(
                [lax.all_gather(part, DATA, axis=0, tiled=True) for part in (stat_0, stat_1)], axis=0
            ).reshape(n_mats, D, D)[own_mat]
        sum_part = lax.dynamic_slice_in_dim(own_sum, basis_start, basis_rows)
        stat_sums = lax.all_gather(sum_part, DATA, axis=0, tiled=True).reshape(n_mats, D, D)
        product = stat_decay * old_product + stat_scale * nn(own_sum, own_basis, highest)
        gram = tn(product, product, highest)
        rows = lax.dynamic_slice_in_dim(product, basis_start, basis_rows)
        rows, gram, own_0 = lax.optimization_barrier((rows, gram, own_0))
        own_mats = jnp.stack([own_0, own_1])
        new_rows = orthogonal_rows(gram, rows)
        new_rows, stat_sums = lax.optimization_barrier((new_rows, stat_sums))
        new_bases = lax.all_gather(new_rows, DATA, axis=0, tiled=True).reshape(soap_bases.shape)
        new_stats = (stat_decay * flat_stats + stat_scale * stat_sums).reshape(soap_stats.shape)

        clipped = own_mats * factor
        basis_lo = jnp.take(soap_bases, lo, axis=1)
        basis_hi = jnp.take(soap_bases, hi, axis=1)

        def by_kind(form, value):
            first = jnp.einsum(form, basis_lo, value, precision=highest)
            second = jnp.einsum(form, basis_hi, value, precision=highest)
            return jnp.where(in_lo[None, None, :], first, second)

        turned = by_kind("lij,lci->ljc", clipped)
        new_mats_first = beta_one * mats_first + (1.0 - beta_one) * turned
        new_mats_second = beta_two * mats_second + (1.0 - beta_two) * turned * turned
        heading = (
            new_mats_first
            / (1.0 - beta_one**STEP)
            / (jnp.sqrt(new_mats_second / (1.0 - beta_two**STEP)) + eps_adam)
        )
        direction = by_kind("lij,ljc->lic", heading)
        new_mats = layer_mats - learn_rate * (direction + decay_weight * layer_mats)
        new_tables, new_tables_first, new_tables_second = adam_update(
            vocab_tables, jnp.stack([grad_embed, grad_head]) * factor, tables_first, tables_second
        )
        new_gains, new_gains_first, new_gains_second = adam_update(
            norm_gains, gain_sum * factor, gains_first, gains_second
        )
        return (
            loss_sum,
            mask_count,
            clip_norm,
            new_mats,
            new_mats_first,
            new_mats_second,
            new_bases,
            new_stats,
            new_tables,
            new_tables_first,
            new_tables_second,
            new_gains,
            new_gains_first,
            new_gains_second,
        )

    return shards


def solution(mesh):
    n_dp, n_fs = mesh.shape["dp"], mesh.shape["fsdp"]
    n_x = 2 ** ((n_dp.bit_length() - 1) // 2)
    fine = Mesh(mesh.devices.reshape(n_dp // n_x, n_x, n_fs // 2, 2), ("z", "x", "y", "c"))
    rows, row = P(DATA, None), P(DATA)
    mats, tables = P(None, None, OWNERS), P(None, OWNERS, None)
    return jax.shard_map(
        make_shards(dict(fine.shape)),
        mesh=fine,
        in_specs=(rows, rows, row, rows, mats, mats, mats, P(), P(), tables, tables, tables, P(), P(), P()),
        out_specs=(P(), P(), P(), mats, mats, mats, P(), P(), tables, tables, tables, P(), P(), P()),
        check_vma=False,
    )
```

```python
import jax
import jax.numpy as jnp
import numpy as np
from jax import lax
from jax.experimental import pallas as pl
from jax.experimental.pallas import tpu as pltpu
from jax.sharding import Mesh
from jax.sharding import PartitionSpec as P

D = 768
HEADS = 12
HD = 64
FF = 2048
V = 32000
LAYERS = 2
ROW = 1024
SLOTS = 256
BINS = 8
STEP = 10
WIDE = 9216
KINDS = 4
BOUNDS = (0, 3 * D, 4 * D, 4 * D + 2 * FF, WIDE)
CAP = 40
PAIR = 2 * HD
PAIRS = D // PAIR
BLOCK = 256
VMEM_CAP = 56 * 2**20
STEPS = 128
LIGHT = pl.CostEstimate(flops=1000, bytes_accessed=1000, transcendentals=0)
TILE = 8

bf16 = jnp.bfloat16
f32 = jnp.float32
highest = lax.Precision.HIGHEST
high = lax.Precision.HIGH
learn_rate = 0.05
beta_one = 0.9
beta_two = 0.95
eps_adam = 1e-08
decay_weight = 0.1
stat_decay = 0.95
clip_limit = 0.05
norm_eps = 1e-05

OWNERS = ("y", "c", "z", "x")
DATA = ("z", "x", "y", "c")
DP = ("z", "x")
FS = ("y", "c")
HEAD_GROUP = ("z", "y", "c")


def dot(a, b, dims, precision=None):
    return lax.dot_general(a, b, (dims, ((), ())), precision=precision, preferred_element_type=f32)


def nn(a, b, precision=None):
    return dot(a, b, ((1,), (0,)), precision)


def nt(a, b, precision=None):
    return dot(a, b, ((1,), (1,)), precision)


def tn(a, b, precision=None):
    return dot(a, b, ((0,), (0,)), precision)


def rms_scale(values, gain):
    return values * lax.rsqrt(jnp.mean(values * values, axis=-1, keepdims=True) + norm_eps) * gain


def silu_up(gate, up):
    return jax.nn.silu(gate) * up


def mm(a, b, ca, cb):
    return lax.dot_general(a, b, (((ca,), (cb,)), ((), ())), preferred_element_type=f32)


def rotate(x, cosine, sine, low_half):
    other = jnp.where(low_half, pltpu.roll(x, PAIR - HD // 2, 1), pltpu.roll(x, HD // 2, 1))
    return x * cosine + other * sine


def lane_masks():
    lane = lax.broadcasted_iota(jnp.int32, (1, PAIR), 1)
    return lane % HD < HD // 2, (lane < HD, lane >= HD)


def attend_kernel(q_ref, k_ref, v_ref, cq_ref, sq_ref, ck_ref, sk_ref, docq_ref, dock_ref,
                  out_ref, qs_ref, kt_ref, vb_ref, lse_ref):
    low_half, own = lane_masks()
    queries = rotate(q_ref[...], cq_ref[...], sq_ref[...], low_half).astype(bf16)
    qs_ref[...] = queries * jnp.asarray(HD ** (-0.5), bf16)
    keys = rotate(k_ref[...], ck_ref[...], sk_ref[...], low_half).astype(bf16)
    kt_ref[...] = keys
    values = v_ref[...]
    vb_ref[...] = values.astype(bf16)
    values_t = values.T.astype(bf16)
    dock = jnp.concatenate([dock_ref[...]] * (BLOCK // 128), axis=1)
    for at in range(0, q_ref.shape[0], BLOCK):
        rows = slice(at, at + BLOCK)
        same = dock == docq_ref[:, rows]
        outs = []
        for h in range(2):
            scores = mm(jnp.where(own[h], keys, 0), qs_ref[rows, :], 1, 1)
            scores = jnp.where(same, scores, -1000000000.0)
            top = jnp.max(scores, axis=0, keepdims=True)
            soft = jnp.exp(scores - top)
            total = jnp.sum(soft, axis=0, keepdims=True)
            lse_ref[0, h : h + 1, rows] = top + jnp.log(total)
            soft = (soft * (1.0 / total)).astype(bf16)
            outs.append(mm(values_t[h * HD : (h + 1) * HD], soft, 1, 0))
        out_ref[rows, :] = jnp.concatenate(outs, axis=0).T.astype(bf16)


def attend_back_kernel(qs_ref, k_ref, v_ref, g_ref, lse_ref, cq_ref, sq_ref, ck_ref, sk_ref, docq_ref, dock_ref,
                       dq_ref, dk_ref, dv_ref, dk_sum, dv_sum):
    low_half, own = lane_masks()
    keys, values = k_ref[...], v_ref[...]
    keys_t = keys.astype(f32).T.astype(bf16)
    dock = jnp.concatenate([dock_ref[...]] * (BLOCK // 128), axis=1)
    for at in range(0, qs_ref.shape[0], BLOCK):
        rows = slice(at, at + BLOCK)
        same = dock == docq_ref[:, rows]
        queries, grad = qs_ref[rows, :], g_ref[rows, :]
        back = []
        for h in range(2):
            scores = mm(jnp.where(own[h], keys, 0), queries, 1, 1)
            soft = jnp.exp(jnp.where(same, scores, -1000000000.0) - lse_ref[0, h : h + 1, rows])
            grad_soft = mm(jnp.where(own[h], values, 0), grad, 1, 1)
            delta = jnp.sum(soft * grad_soft, axis=0, keepdims=True)
            grad_scores = (soft * (grad_soft - delta)).astype(bf16)
            dv = mm(soft.astype(bf16), jnp.where(own[h], grad, 0), 1, 0)
            dk = mm(grad_scores, jnp.where(own[h], queries, 0), 1, 0)
            if at == 0 and h == 0:
                dv_sum[...] = dv
                dk_sum[...] = dk
            else:
                dv_sum[...] += dv
                dk_sum[...] += dk
            back.append(mm(keys_t[h * HD : (h + 1) * HD], grad_scores, 1, 0))
        dq = jnp.concatenate(back, axis=0).T * HD ** (-0.5)
        dq_ref[rows, :] = rotate(dq, cq_ref[rows, :], -sq_ref[rows, :], low_half).astype(bf16)
    dk_ref[...] = rotate(dk_sum[...], ck_ref[...], -sk_ref[...], low_half).astype(bf16)
    dv_ref[...] = dv_sum[...].astype(bf16)


def column(rows, shift=0):
    return pl.BlockSpec((rows, PAIR), lambda h: (0, h + shift))


def whole(shape):
    return pl.BlockSpec(shape, lambda h: (0,) * len(shape))


def stat_spec(rows):
    return pl.BlockSpec((1, 2, rows), lambda h: (h, 0, 0))


def attend(q, kv, turn_q, turn_k, doc_q, doc_k):
    n_q, n_k = q.shape[0], kv.shape[0]
    low = jax.ShapeDtypeStruct((n_q, D), bf16)
    low_k = jax.ShapeDtypeStruct((n_k, D), bf16)
    return pl.pallas_call(
        attend_kernel,
        grid=(PAIRS,),
        in_specs=[column(n_q), column(n_k), column(n_k, PAIRS)]
        + [whole((n_q, PAIR))] * 2 + [whole((n_k, PAIR))] * 2 + [whole((1, n_q)), whole((n_k, 128))],
        out_specs=[column(n_q), column(n_q), column(n_k), column(n_k), stat_spec(n_q)],
        out_shape=[low, low, low_k, low_k, jax.ShapeDtypeStruct((PAIRS, 2, n_q), f32)],
        compiler_params=pltpu.CompilerParams(vmem_limit_bytes=VMEM_CAP),
        cost_estimate=LIGHT,
        name="attend",
    )(q, kv, kv, *turn_q, *turn_k, doc_q, doc_k)


def attend_back(qs, k, v, grad, lse, turn_q, turn_k, doc_q, doc_k):
    n_q, n_k = qs.shape[0], k.shape[0]
    low = jax.ShapeDtypeStruct((n_q, D), bf16)
    low_k = jax.ShapeDtypeStruct((n_k, D), bf16)
    return pl.pallas_call(
        attend_back_kernel,
        grid=(PAIRS,),
        in_specs=[column(n_q), column(n_k), column(n_k), column(n_q), stat_spec(n_q)]
        + [whole((n_q, PAIR))] * 2 + [whole((n_k, PAIR))] * 2 + [whole((1, n_q)), whole((n_k, 128))],
        out_specs=[column(n_q), column(n_k), column(n_k)],
        out_shape=[low, low_k, low_k],
        scratch_shapes=[pltpu.VMEM((n_k, PAIR), f32)] * 2,
        compiler_params=pltpu.CompilerParams(vmem_limit_bytes=VMEM_CAP),
        cost_estimate=LIGHT,
        name="attend_back",
    )(qs, k, v, grad, lse, *turn_q, *turn_k, doc_q, doc_k)


def pair_tables(position):
    half = HD // 2
    frequency = 10000.0 ** (-jnp.arange(half, dtype=f32) / half)
    angles = position[:, None].astype(f32) * frequency
    cosine, sine = jnp.cos(angles), jnp.sin(angles)
    return jnp.concatenate([cosine] * 4, axis=1), jnp.concatenate([-sine, sine] * 2, axis=1)


def fm(a, b, ca, cb):
    return lax.dot_general(a, b, (((ca,), (cb,)), ((), ())), precision=highest, preferred_element_type=f32)


def inverse_factor(block):
    row_at = lax.broadcasted_iota(jnp.int32, (STEPS, STEPS), 0)
    col_at = lax.broadcasted_iota(jnp.int32, (STEPS, STEPS), 1)
    eye = jnp.where(row_at == col_at, 1.0, 0.0).astype(f32)
    sub = lax.broadcasted_iota(jnp.int32, (TILE, 1), 0)
    n = STEPS // TILE
    left = [block[i * TILE : (i + 1) * TILE] for i in range(n)]
    right = [eye[i * TILE : (i + 1) * TILE] for i in range(n)]
    for j in range(STEPS):
        at, within = divmod(j, TILE)
        row = left[at][within : within + 1]
        scale = 1.0 / row[:, j : j + 1]
        row = row * scale
        mate = right[at][within : within + 1] * scale
        for i in range(at, n):
            column = left[i][:, j : j + 1]
            if i == at:
                column = jnp.where(sub > within, column, 0.0)
            left[i] = left[i] - column * row
            right[i] = right[i] - column * mate
    upper = jnp.concatenate(left, axis=0)
    pivots = jnp.sum(jnp.where(row_at == col_at, upper, 0.0), axis=1, keepdims=True)
    return jnp.concatenate(right, axis=0) * lax.rsqrt(pivots)


def orthogonal_kernel(gram_ref, rows_ref, out_ref, rest_ref):
    rest_ref[...] = gram_ref[...]
    out_ref[...] = rows_ref[...]
    lane = lax.broadcasted_iota(jnp.int32, (1, D), 1)

    def body(b, _):
        start = pl.multiple_of(b * STEPS, STEPS)
        here = pl.ds(start, STEPS)
        inverse = inverse_factor(rest_ref[here, here])
        upper = jnp.where(lane >= start + STEPS, fm(inverse, rest_ref[here, :], 1, 0), 0.0)
        done = fm(out_ref[:, here], inverse, 1, 1)
        out_ref[...] -= fm(done, upper, 1, 0)
        out_ref[:, here] = done
        rest_ref[...] -= fm(upper, upper, 0, 0)
        return 0

    lax.fori_loop(0, D // STEPS, body, 0)


def orthogonal_rows(gram, rows):
    return pl.pallas_call(
        orthogonal_kernel,
        out_shape=jax.ShapeDtypeStruct(rows.shape, f32),
        in_specs=[pl.BlockSpec(memory_space=pltpu.VMEM)] * 2,
        out_specs=pl.BlockSpec(memory_space=pltpu.VMEM),
        scratch_shapes=[pltpu.VMEM((D, D), f32)],
        compiler_params=pltpu.CompilerParams(vmem_limit_bytes=40 * 2**20),
        cost_estimate=pl.CostEstimate(flops=2 * 10**11, bytes_accessed=8 * D * D, transcendentals=0),
        name="orthogonal_rows",
    )(gram, rows)


def adam_update(weight, grad, first, second):
    first = beta_one * first + (1.0 - beta_one) * grad
    second = beta_two * second + (1.0 - beta_two) * grad * grad
    heading = (
        first / (1.0 - beta_one**STEP) / (jnp.sqrt(second / (1.0 - beta_two**STEP)) + eps_adam)
    )
    return (weight - learn_rate * (heading + decay_weight * weight), first, second)


def parts_of(weights):
    return (
        weights[: 3 * D],
        weights[3 * D : 4 * D],
        weights[4 * D : 4 * D + 2 * FF],
        weights[4 * D + 2 * FF :],
    )


def layer_forward(residual, slots, weights, gains, doc, tables):
    w_qkv, w_out, w_gu, w_down = parts_of(weights)
    normed = rms_scale(residual, gains[0]).astype(bf16)
    if slots is None:
        rows_in, normed_q, doc_q, tables_q = residual, normed, doc[0], tables
    else:
        pick, doc_q, tables_q = slots
        rows_in = nn(pick.astype(f32), residual, highest)
        normed_q = nn(pick, normed).astype(bf16)
    attended, *kept = attend(
        nt(normed_q, w_qkv[:D]), nt(normed, w_qkv[D:]), tables_q, tables, doc_q, doc[1]
    )
    middle = rows_in + nt(attended, w_out)
    normed_ffn = rms_scale(middle, gains[1]).astype(bf16)
    gate_up = nt(normed_ffn, w_gu)
    activated = silu_up(gate_up[:, :FF], gate_up[:, FF:]).astype(bf16)
    result = middle + nn(activated, w_down)
    saved = (residual, normed, normed_q, kept, attended, middle, normed_ffn, gate_up, activated)
    return result, saved


def ffn_back(grad_out, saved, weights, gains, cut, between, emit):
    _, _, w_gu, w_down = parts_of(weights)
    _, _, _, _, attended, middle, normed_ffn, gate_up, activated = saved
    grad_low = grad_out.astype(bf16)
    grad_down = tn(activated, grad_low)
    grad_act = nt(grad_low, w_down)
    _, pull_act = jax.vjp(silu_up, gate_up[:, :FF], gate_up[:, FF:])
    grad_gate_up = jnp.concatenate(pull_act(grad_act), axis=1).astype(bf16)
    grad_gate_up, grad_down = between((grad_gate_up, grad_down))
    grad_gu_end = tn(grad_gate_up[:, cut:], normed_ffn)
    grad_gate_up = emit(grad_gate_up, grad_gu_end, grad_down)
    grad_gu = [tn(grad_gate_up[:, :cut], normed_ffn), grad_gu_end]
    _, pull_ffn = jax.vjp(rms_scale, middle, gains[1])
    grad_middle, grad_gain = pull_ffn(nn(grad_gate_up, w_gu))
    grad_middle = grad_out + grad_middle
    branch = grad_middle.astype(bf16)
    return grad_middle, branch, tn(branch, attended), grad_gu, grad_down, grad_gain


def attention_back(grad_middle, branch, saved, slots, weights, gains, doc, tables, before, between):
    w_qkv, w_out, _, _ = parts_of(weights)
    residual, normed, normed_q, kept, _, _, _, _, _ = saved
    grad_att = before(nn(branch, w_out).astype(bf16))
    if slots is None:
        doc_q, tables_q = doc[0], tables
    else:
        pick, doc_q, tables_q = slots
    qs, k, v, lse = kept
    grads = attend_back(qs, k, v, grad_att, lse, tables_q, tables, doc_q, doc[1])
    grad_q, grad_k, grad_v = between(grads)
    grad_qkv = jnp.concatenate([tn(grad_q, normed_q), tn(grad_k, normed), tn(grad_v, normed)], 0)
    grad_in = nn(grad_k, w_qkv[D : 2 * D]) + nn(grad_v, w_qkv[2 * D :])
    grad_in_q = nn(grad_q, w_qkv[:D])
    if slots is not None:
        grad_in_q = tn(pick.astype(f32), grad_in_q, highest)
        grad_middle = tn(pick.astype(f32), grad_middle, highest)
    _, pull_att = jax.vjp(rms_scale, residual, gains[0])
    grad_residual, grad_gain = pull_att(grad_in + grad_in_q)
    return grad_middle + grad_residual, grad_qkv, grad_gain


def make_shards(sizes):
    n_z, n_x, n_y, n_c = (sizes[a] for a in ("z", "x", "y", "c"))
    n_dp, n_fs = n_z * n_x, n_y * n_c
    n_dev = n_dp * n_fs
    per = V // n_dev
    cols = WIDE // n_dev
    span = WIDE // n_fs
    n_mats = LAYERS * KINDS
    stat_rows = D // n_dp
    sharing = n_dev // n_mats
    basis_rows = D // sharing
    kind_of = np.searchsorted(np.array(BOUNDS[1:]), np.arange(WIDE), side="right")
    kind_lo = [int(kind_of[f * span]) for f in range(n_fs)]
    kind_hi = [int(kind_of[(f + 1) * span - 1]) for f in range(n_fs)]
    slots_all = n_dev * CAP
    shape = (n_z, n_x, n_y, n_c)
    paired = n_x == 2 and n_y == 2 and n_c == 2 and n_dp == n_mats

    def moved(value, target):
        pairs = []
        for source in np.ndindex(n_z, n_x, n_y, n_c):
            dest = target(*source)
            if dest is not None:
                pairs.append((np.ravel_multi_index(source, shape), np.ravel_multi_index(dest, shape)))
        return lax.ppermute(value, DATA, [(int(s), int(d)) for s, d in pairs])

    def take(value, axis, at):
        return lax.dynamic_index_in_dim(value, at, axis, keepdims=False)

    def z_line(value, inside):
        at = lax.axis_index("z")
        up, down = 0.0, 0.0
        for k in range(n_z - 1, 0, -1):
            up = value[jnp.minimum(at + k, n_z - 1)] + up
            down = value[jnp.maximum(at - k, 0)] + down
            up, down = yield (
                (up, lambda z, x, y, c: (z + 1, x, y, c) if inside(y, c) and z + k < n_z else None),
                (down, lambda z, x, y, c: (z - 1, x, y, c) if inside(y, c) and z >= k else None),
            )
        return value[at] + up + down

    def sum_all(value):
        c, y, x = lax.axis_index("c"), lax.axis_index("y"), lax.axis_index("x")
        rows = value.shape[-2] // 2

        def by_x(z, x, y, c):
            return z, 1 - x, y, c

        def by_y(z, x, y, c):
            return z, x, 1 - y, c

        kept = take(value, 1, c)
        (sent,) = yield ((take(value, 1, 1 - c), lambda z, x, y, c: (z, x, y, 1 - c)),)
        first = kept[..., :rows, :] + sent[..., :rows, :]
        second = kept[..., rows:, :] + sent[..., rows:, :]
        sent_x, sent_y = yield ((take(first, 2, 1 - x), by_x), (take(second, 0, 1 - y), by_y))
        first, second = take(first, 2, x) + sent_x, take(second, 0, y) + sent_y
        sent_y, sent_x = yield ((take(first, 0, 1 - y), by_y), (take(second, 1, 1 - x), by_x))
        first, second = take(first, 0, y) + sent_y, take(second, 1, x) + sent_x
        return (yield from z_line(jnp.concatenate([first, second], axis=-2), lambda y, c: True))

    class Lane:
        def __init__(self, steps):
            self.steps, self.done, self.flying = steps, False, []
            self.asks = next(steps)

        def land(self, landed):
            try:
                self.asks = self.steps.send(landed)
            except StopIteration as end:
                self.done, self.result = True, end.value

    def start(value, *lanes):
        lanes = [lane for lane in lanes if not lane.done]
        operands = [[operand for operand, _ in lane.asks] for lane in lanes]
        value, operands = lax.optimization_barrier((value, operands))
        for lane, each in zip(lanes, operands):
            lane.flying = [moved(operand, target) for operand, (_, target) in zip(each, lane.asks)]
        return value

    def tick(value, *lanes):
        lanes = [lane for lane in lanes if not lane.done]
        value, landed = lax.optimization_barrier((value, [lane.flying for lane in lanes]))
        for lane, each in zip(lanes, landed):
            lane.land(each)
        return start(value, *lanes)

    half = cols // 2
    has = [[(kind_of.reshape(n_fs, n_dp, cols) == kind)[f].any(axis=1) for f in range(n_fs)] for kind in range(KINDS)]
    merges = [n_fs == 4 and not any((has[k][y] & has[k][2 + y]).any() for y in range(2)) for k in range(KINDS)]
    work_axes = ("y", "z", "x", "c")

    def to_work(own):
        y, c = lax.axis_index("y"), lax.axis_index("c")
        pieces = own.reshape(1, 2, half, D) * (jnp.arange(2)[:, None, None, None] == c)
        got = lax.all_to_all(pieces.reshape(-1, D), FS, 0, 0, tiled=True).reshape(2, 2, half, D)
        return take(got, 1, y).reshape(-1, D)

    def from_work(work):
        y, c = lax.axis_index("y"), lax.axis_index("c")
        pieces = work.reshape(2, 1, half, D) * (jnp.arange(2)[None, :, None, None] == y)
        got = lax.all_to_all(pieces.reshape(-1, D), FS, 0, 0, tiled=True).reshape(2, 2, half, D)
        return take(got, 0, c).reshape(-1, D)

    def share_stat(columns):
        part = tn(columns, columns, highest)
        c = lax.axis_index("c")
        halves = part.reshape(2, D // 2, D)
        mine = take(halves, 0, c) + moved(take(halves, 0, 1 - c), lambda z, x, y, c: (z, x, y, 1 - c))
        mine = mine + moved(mine, lambda z, x, y, c: (z, x, 1 - y, c))
        other = moved(mine, lambda z, x, y, c: (z, x, y, 1 - c))
        return jnp.where(c == 0, jnp.concatenate([mine, other], 0), jnp.concatenate([other, mine], 0))

    def shards(
        token_ids,
        mask_flags,
        time_bins,
        doc_lengths,
        layer_mats,
        mats_first,
        mats_second,
        soap_bases,
        soap_stats,
        vocab_tables,
        tables_first,
        tables_second,
        norm_gains,
        gains_first,
        gains_second,
    ):
        tokens, flags, lengths = token_ids[0], mask_flags[0], doc_lengths[0]
        work_mats = layer_mats.astype(bf16).transpose(0, 2, 1)
        work_tables = vocab_tables.astype(bf16)
        spots = jnp.arange(ROW, dtype=jnp.int32)

        ids = jnp.where(flags == 1, V - 1, tokens)
        owner = ids // per
        same_id = ids[:, None] == ids[None, :]
        before = spots[None, :] < spots[:, None]
        is_first = ~jnp.any(same_id & before, axis=1)
        place = jnp.sum(
            (before & is_first[None, :] & (owner[:, None] == owner[None, :])).astype(jnp.int32), axis=1
        )
        place = jnp.sum(jnp.where(same_id & is_first[None, :], place[None, :], 0), axis=1)
        mats_0 = lax.all_gather(work_mats[0], OWNERS, axis=0, tiled=True)
        slot_ids = jnp.arange(slots_all, dtype=jnp.int32)
        row_ids = jnp.arange(per, dtype=jnp.int32)

        def plan(turn_at):
            at = place - turn_at * CAP
            slot = jnp.where((at >= 0) & (at < CAP), owner * CAP + at, -1)
            hit = slot[:, None] == slot_ids[None, :]
            asked = jnp.max(jnp.where(hit, ids[:, None] % per, -1), axis=0).reshape(n_dev, CAP)
            most = jnp.broadcast_to(jnp.max(place), (n_dev, 128 - CAP))
            asked = jnp.concatenate([asked, most], axis=1)
            asked = lax.all_to_all(asked, OWNERS, 0, 0, tiled=True)
            rows = asked[:, :CAP].reshape(-1)[:, None] == row_ids[None, :]
            return hit, rows, jnp.max(asked[:, CAP]) // CAP + 1

        def fetch(hit, rows):
            sent = nn(rows.astype(bf16), work_tables[0]).astype(bf16)
            got = lax.all_to_all(sent, OWNERS, 0, 0, tiled=True)
            return nn(hit.astype(bf16), got)

        def embed_send(hit, grad):
            return tn(hit.astype(f32), grad, high)

        def exchange(sent):
            return lax.all_to_all(sent, OWNERS, 0, 0, tiled=True)

        def embed_sum(rows, got):
            return tn(rows.astype(f32), got, high)

        def fetch_more(turn_at, residual):
            hit, rows, _ = plan(turn_at)
            return residual + fetch(hit, rows)

        def give_more(turn_at, carry):
            total, grad = carry
            hit, rows, _ = plan(turn_at)
            return total + embed_sum(rows, exchange(embed_send(hit, grad))), grad

        hit_0, rows_0, rounds = plan(0)
        residual = fetch(hit_0, rows_0)
        residual = lax.fori_loop(1, rounds, fetch_more, residual)

        at_fs, at_dp = lax.axis_index(FS), lax.axis_index(DP)
        lo = jnp.asarray(kind_lo, jnp.int32)[at_fs]
        hi = jnp.asarray(kind_hi, jnp.int32)[at_fs]
        col_ids = (at_fs * n_dp + lax.axis_index(DP)) * cols + jnp.arange(cols, dtype=jnp.int32)
        kind_ids = sum((col_ids >= b).astype(jnp.int32) for b in BOUNDS[1:-1])
        in_lo = kind_ids == lo

        def stat_scatter(own):
            part = jnp.concatenate(
                [tn(jnp.where(in_lo[:, None], own, 0.0), own, highest), tn(jnp.where(in_lo[:, None], 0.0, own), own, highest)],
                axis=0,
            ).reshape(2, D, D)
            every = jnp.stack(
                [jnp.where(lo == kind, part[0], jnp.where(hi == kind, part[1], 0.0)) for kind in range(KINDS)]
            ).reshape(KINDS * D, D)
            return lax.psum_scatter(every, DATA, scatter_dimension=0, tiled=True)

        ends = jnp.cumsum(lengths)
        passed = spots[:, None] >= ends[None, :]
        doc = jnp.sum(passed.astype(jnp.int32), axis=1)
        position = spots - jnp.sum(jnp.where(passed, lengths[None, :], 0), axis=1)
        tables = pair_tables(position)
        docs = (doc[None, :], jnp.broadcast_to(doc[:, None], (ROW, 128)))

        count = jnp.sum(flags)
        order = jnp.where(flags == 1, jnp.cumsum(flags) - 1, count + jnp.cumsum(1 - flags) - 1)
        at_slot = order[None, :] == jnp.arange(SLOTS, dtype=jnp.int32)[:, None]
        pick = at_slot.astype(bf16)

        def picked(vector):
            return jnp.sum(jnp.where(at_slot, vector[None, :], jnp.zeros((), vector.dtype)), axis=1)

        targets = picked(tokens)
        valid = jnp.arange(SLOTS, dtype=jnp.int32) < count
        code = jnp.where(valid, time_bins[0] + 1, 0)
        slots = (pick, picked(doc)[None, :], pair_tables(picked(position)))

        group_codes = lax.all_gather(jnp.stack([targets, code]), HEAD_GROUP, axis=1, tiled=True)
        residual, group_codes = lax.optimization_barrier((residual, group_codes))
        group_targets, group_codes = group_codes[0], group_codes[1]

        mats_1 = lax.all_gather(work_mats[1], OWNERS, axis=0, tiled=True)
        residual, saved_0 = layer_forward(residual, None, mats_0, norm_gains[0:2], docs, tables)
        if paired:
            x = lax.axis_index("x")
            other = moved(work_tables[1], lambda z, x, y, c: (z, 1 - x, y, c))
            residual, other = lax.optimization_barrier((residual, other))
            head = jnp.concatenate([jnp.where(x == 0, work_tables[1], other), jnp.where(x == 0, other, work_tables[1])], 0)
        else:
            head = lax.all_gather(work_tables[1], "x", axis=0, tiled=True)
        final, saved_1 = layer_forward(residual, slots, mats_1, norm_gains[2:4], docs, tables)

        chosen_full, pull_final = jax.vjp(rms_scale, final, norm_gains[2 * LAYERS])
        states = lax.all_gather(chosen_full.astype(bf16), HEAD_GROUP, axis=0, tiled=True)
        logits = nt(states, head)
        base_shard = lax.axis_index(FS) * n_dp + lax.axis_index("z") * n_x
        vocab_ids = base_shard * per + jnp.arange(n_x * per, dtype=jnp.int32)
        onehot = vocab_ids[None, :] == group_targets[:, None]
        top = jnp.max(logits, axis=1)
        total = jnp.sum(jnp.exp(logits - top[:, None]), axis=1)
        hit_logit = jnp.sum(jnp.where(onehot, logits, 0.0), axis=1)
        parts = jnp.stack([top, total, hit_logit])
        for axes in (FS, "z"):
            each = lax.all_gather(parts, axes, axis=0)
            top = jnp.max(each[:, 0], axis=0)
            parts = jnp.stack(
                [top, jnp.sum(each[:, 1] * jnp.exp(each[:, 0] - top), axis=0), jnp.sum(each[:, 2], axis=0)]
            )
        log_total, target_logit = parts[0] + jnp.log(parts[1]), parts[2]
        weight = jnp.where(group_codes > 0, BINS / jnp.maximum(group_codes, 1).astype(f32), 0.0)
        own_start = lax.axis_index(HEAD_GROUP) * SLOTS
        loss_part = jnp.sum(
            lax.dynamic_slice_in_dim(weight * (log_total - target_logit), own_start, SLOTS)
        )
        grad_logits = (
            weight[:, None] * (jnp.exp(logits - log_total[:, None]) - onehot.astype(f32))
        ).astype(bf16)
        grad_states = lax.psum_scatter(nn(grad_logits, head), HEAD_GROUP, scatter_dimension=0, tiled=True)
        head_part = tn(grad_logits, states)
        grad_states, head_part = lax.optimization_barrier((grad_states, head_part))
        if paired:
            head_part = head_part.reshape(n_x, per, D)
            head_sent = moved(take(head_part, 0, 1 - x), lambda z, x, y, c: (z, 1 - x, y, c))
        else:
            grad_head = lax.psum_scatter(head_part, "x", scatter_dimension=0, tiled=True)
        grad_final, grad_final_gain = pull_final(grad_states)

        cut = WIDE // 2 - 4 * D

        def same(value):
            return value

        def keep(value, *others):
            return value

        def stat_of_owner(work_0, work_1):
            y, c = lax.axis_index("y"), lax.axis_index("c")
            starts = ((jnp.arange(2) * 2 + y) * n_dp + at_dp) * cols + c * half
            work_cols = (starts[:, None] + jnp.arange(half)[None, :]).reshape(-1)
            work_kinds = sum((work_cols >= b).astype(jnp.int32) for b in BOUNDS[1:-1])
            to_owner = []
            for work in (work_0, work_1):
                for kind in range(KINDS):
                    mine = jnp.where((work_kinds == kind)[:, None], work, 0.0)
                    to_owner.append(mine[:half] + mine[half:] if merges[kind] else mine)
            most_rows = max(piece.shape[0] for piece in to_owner)
            to_owner = [jnp.pad(piece, ((0, most_rows - piece.shape[0]), (0, 0))) for piece in to_owner]
            columns = lax.all_to_all(jnp.stack(to_owner), DP, 0, 0, tiled=True)
            return share_stat(columns.reshape(-1, D))

        own_mat = at_dp * n_mats // n_dp
        flat_stats = soap_stats.reshape(n_mats, D, D)
        own_basis = soap_bases.reshape(n_mats, D, D)[own_mat]
        old_product = nn(flat_stats[own_mat], own_basis, highest)

        def rows_sum(rows):
            return lax.psum_scatter(rows, work_axes if paired else OWNERS, scatter_dimension=0, tiled=True)

        middle_1, branch, out_1, gu_1, down_1, gain_f1 = ffn_back(
            grad_final, saved_1, mats_1, norm_gains[2:4], cut, same, keep
        )
        grad_1, qkv_1, gain_a1 = attention_back(
            middle_1, branch, saved_1, slots, mats_1, norm_gains[2:4], docs, tables, same, same
        )
        if paired:
            all_1 = jnp.concatenate([qkv_1, out_1, *gu_1, down_1], axis=0)
            lane_1 = Lane(sum_all(all_1.reshape(n_y, n_c, n_z, n_x, cols, D)))
            grad_1, head_sent = lax.optimization_barrier((grad_1, head_sent))
            grad_head = take(head_part, 0, x) + head_sent
            grad_1 = start(grad_1, lane_1)
            early_0 = None

            def emit_early(value, gu_end, down):
                nonlocal early_0
                value, early_0 = lax.optimization_barrier((value, jnp.concatenate([gu_end, down], axis=0)))
                early_0 = rows_sum(early_0)
                return value

            middle_0, branch, out_0, gu_0, down_0, gain_f0 = ffn_back(
                grad_1, saved_0, mats_0, norm_gains[0:2], cut, lambda v: tick(v, lane_1), emit_early
            )
            grad_0, qkv_0, gain_a0 = attention_back(
                middle_0, branch, saved_0, None, mats_0, norm_gains[0:2], docs, tables, same, same
            )
            late_0 = jnp.concatenate([qkv_0, out_0, gu_0[0]], axis=0)
            grad_0, late_0 = tick((grad_0, late_0), lane_1)
            grad_0, late_0, early_0 = lax.optimization_barrier((grad_0, late_0, early_0))
            late_0 = rows_sum(late_0)
            sent = embed_send(hit_0, grad_0)
            sent = tick(sent, lane_1)
            while not lane_1.done:
                tick((), lane_1)
            own_1 = lane_1.result
            work_1 = to_work(own_1)
            work_1, late_0, sent, old_product = lax.optimization_barrier((work_1, late_0, sent, old_product))
            embed_got = exchange(sent)
            work_0 = jnp.concatenate([late_0, early_0], axis=0)
            own_sum = stat_of_owner(work_0, work_1)
            own_sum, embed_got = lax.optimization_barrier((own_sum, embed_got))
            own_0 = from_work(work_0)
        else:
            own_1 = rows_sum(jnp.concatenate([qkv_1, out_1, *gu_1, down_1], axis=0))
            middle_0, branch, out_0, gu_0, down_0, gain_f0 = ffn_back(
                grad_1, saved_0, mats_0, norm_gains[0:2], cut, same, keep
            )
            grad_0, qkv_0, gain_a0 = attention_back(
                middle_0, branch, saved_0, None, mats_0, norm_gains[0:2], docs, tables, same, same
            )
            own_0 = rows_sum(jnp.concatenate([qkv_0, out_0, *gu_0, down_0], axis=0))
            embed_got = exchange(embed_send(hit_0, grad_0))
            stat_0, stat_1 = stat_scatter(own_0), stat_scatter(own_1)
        grad_embed = embed_sum(rows_0, embed_got)
        grad_embed, _ = lax.fori_loop(1, rounds, give_more, (grad_embed, grad_0))

        gain_part = jnp.stack([gain_a0, gain_f0, gain_a1, gain_f1, grad_final_gain])
        held = jnp.concatenate([work_0, work_1] if paired else [own_0, own_1], axis=0)
        square = jnp.sum(held * held) + jnp.sum(grad_embed * grad_embed) + jnp.sum(grad_head * grad_head)
        scalars = jnp.stack([square, loss_part, count.astype(f32)])
        small = jnp.concatenate([gain_part, jnp.broadcast_to(scalars[:, None], (3, D))], axis=0)
        if paired:
            own_sum, small = lax.optimization_barrier((own_sum, small))
        small = jnp.sum(lax.all_gather(small, ("x", "y", "c"), axis=0), axis=0)
        small = jnp.sum(lax.all_gather(small, "z", axis=0), axis=0)
        gain_sum = small[: 2 * LAYERS + 1]
        square_sum, loss_sum, mask_count = (small[2 * LAYERS + 1 + i, 0] for i in range(3))
        clip_norm = jnp.sqrt(square_sum + jnp.sum(gain_sum * gain_sum)) / mask_count
        factor = jnp.minimum(1.0, clip_limit / clip_norm) / mask_count

        stat_scale = (1.0 - stat_decay) * (factor * factor)
        linear = at_dp * n_fs + at_fs
        basis_start = (linear % sharing) * basis_rows
        if not paired:
            own_sum = jnp.concatenate(
                [lax.all_gather(part, DATA, axis=0, tiled=True) for part in (stat_0, stat_1)], axis=0
            ).reshape(n_mats, D, D)[own_mat]
        sum_part = lax.dynamic_slice_in_dim(own_sum, basis_start, basis_rows)
        stat_sums = lax.all_gather(sum_part, DATA, axis=0, tiled=True).reshape(n_mats, D, D)
        product = stat_decay * old_product + stat_scale * nn(own_sum, own_basis, highest)
        gram = tn(product, product, highest)
        rows = lax.dynamic_slice_in_dim(product, basis_start, basis_rows)
        new_rows = orthogonal_rows(gram, rows)
        new_rows, stat_sums, own_0 = lax.optimization_barrier((new_rows, stat_sums, own_0))
        own_mats = jnp.stack([own_0, own_1])
        new_bases = lax.all_gather(new_rows, DATA, axis=0, tiled=True).reshape(soap_bases.shape)
        new_stats = (stat_decay * flat_stats + stat_scale * stat_sums).reshape(soap_stats.shape)

        clipped = own_mats * factor
        basis_lo = jnp.take(soap_bases, lo, axis=1)
        basis_hi = jnp.take(soap_bases, hi, axis=1)

        def by_kind(form, value):
            first = jnp.einsum(form, basis_lo, value, precision=highest)
            second = jnp.einsum(form, basis_hi, value, precision=highest)
            return jnp.where(in_lo[None, None, :], first, second)

        turned = by_kind("lij,lci->ljc", clipped)
        new_mats_first = beta_one * mats_first + (1.0 - beta_one) * turned
        new_mats_second = beta_two * mats_second + (1.0 - beta_two) * turned * turned
        heading = (
            new_mats_first
            / (1.0 - beta_one**STEP)
            / (jnp.sqrt(new_mats_second / (1.0 - beta_two**STEP)) + eps_adam)
        )
        direction = by_kind("lij,ljc->lic", heading)
        new_mats = layer_mats - learn_rate * (direction + decay_weight * layer_mats)
        new_tables, new_tables_first, new_tables_second = adam_update(
            vocab_tables, jnp.stack([grad_embed, grad_head]) * factor, tables_first, tables_second
        )
        new_gains, new_gains_first, new_gains_second = adam_update(
            norm_gains, gain_sum * factor, gains_first, gains_second
        )
        return (
            loss_sum,
            mask_count,
            clip_norm,
            new_mats,
            new_mats_first,
            new_mats_second,
            new_bases,
            new_stats,
            new_tables,
            new_tables_first,
            new_tables_second,
            new_gains,
            new_gains_first,
            new_gains_second,
        )

    return shards


def solution(mesh):
    n_dp, n_fs = mesh.shape["dp"], mesh.shape["fsdp"]
    n_x = 2 ** ((n_dp.bit_length() - 1) // 2)
    fine = Mesh(mesh.devices.reshape(n_dp // n_x, n_x, n_fs // 2, 2), ("z", "x", "y", "c"))
    rows, row = P(DATA, None), P(DATA)
    mats, tables = P(None, None, OWNERS), P(None, OWNERS, None)
    return jax.shard_map(
        make_shards(dict(fine.shape)),
        mesh=fine,
        in_specs=(rows, rows, row, rows, mats, mats, mats, P(), P(), tables, tables, tables, P(), P(), P()),
        out_specs=(P(), P(), P(), mats, mats, mats, P(), P(), tables, tables, tables, P(), P(), P()),
        check_vma=False,
    )
```
